256 devices in a mesh: dp: 2 (over core), tensor: 8 (over z), context: 16 (over y, x).
Axes of the slice: x: 4, y: 4, z: 8, core: 2. Of those that a mesh axis runs over, the one named last changes fastest.
Arguments:
- x_raw: bfloat16 [8192, 8192], P(('dp', 'context'), 'tensor'), parts along dimension 0, may hold values from -6 to 6
- b_raw: bfloat16 [8192, 1024], P(('dp', 'context'), 'tensor'), parts along dimension 0, may hold values from -6 to 6
- c_raw: bfloat16 [8192, 1024], P(('dp', 'context'), 'tensor'), parts along dimension 0, may hold values from -6 to 6
- dt_raw: bfloat16 [128, 8192], P('tensor', ('dp', 'context')), parts along dimension 1, may hold values from -3.5 to 12
- dt_bias: float32 [128], P('tensor'), may hold values from -8 to -7
- a_log: float32 [128], P('tensor'), may hold values from -4.5 to 4.5
- skip_gain: float32 [128], P('tensor'), may hold values from 0.5 to 1.5
- conv_x: float32 [4, 8192], P(None, 'tensor'), may hold values from -2 to 2
- conv_b: float32 [4, 1024], P(None, 'tensor'), may hold values from -2 to 2
- conv_c: float32 [4, 1024], P(None, 'tensor'), may hold values from -2 to 2
- grad_y: bfloat16 [8192, 8192], P(('dp', 'context'), 'tensor'), parts along dimension 0, may hold values from -6 to 6
Outputs:
- y_out: float32 [8192, 8192], P(('dp', 'context'), 'tensor'), parts along dimension 0
- grad_x: float32 [8192, 8192], P(('dp', 'context'), 'tensor'), parts along dimension 0
- grad_b: float32 [8192, 1024], P(('dp', 'context'), 'tensor'), parts along dimension 0
- grad_c: float32 [8192, 1024], P(('dp', 'context'), 'tensor'), parts along dimension 0
- grad_dt: float32 [128, 8192], P('tensor', ('dp', 'context')), parts along dimension 1
The draws below stay inside these ranges and needn't reach their ends.
There are 2 independent parts, one for each index of `dp`. The reference program is written for one: setup_inputs(seed, part) draws one part's arguments, and reference() takes and returns one part's arrays. A program takes and returns all parts, laid end to end along the dimension named above; an argument that names none is the same for every part. Nothing has to cross between parts.
All inputs are finite; a program needn't handle non-finite values.
Results may differ from the reference program's by a relative error of at most 0.0003.
Values may be sent and summed in bfloat16 or wider, within the bound.
No kernel may reach another device: no remote copies, remote signals or barrier semaphores. Data moves between devices by JAX's collectives and lax.ppermute only.
A program may use at most 64 MiB of HBM per device.

```python
import math
import jax
import jax.numpy as jnp
from jax import lax

HEADS = 128
HEAD_DIM = 64
STATE = 128
GROUPS = 8
SPAN = 256
CONV = 4
TOK_DEV = 256
ROLLOUT_TOKENS = 4096


base_step = 0.00055


def draw_a_log(key, part):
    key = jax.random.fold_in(key, 11)
    pick_key, kept_key, fast_key = jax.random.split(key, 3)
    slow_share = 50
    kept_low = 0.3
    is_slow = jax.random.randint(pick_key, (HEADS,), 0, 100) < slow_share
    kept_total = jnp.exp(jax.random.uniform(kept_key, (HEADS,), jnp.float32, math.log(kept_low), math.log(2.0)))
    fast_rate = jnp.exp(jax.random.uniform(fast_key, (HEADS,), jnp.float32, math.log(4.0 / ROLLOUT_TOKENS), math.log(0.035)))
    per_token = jnp.where(is_slow, kept_total / ROLLOUT_TOKENS, fast_rate)
    return jnp.clip(jnp.log(per_token / base_step), -4.5, 4.5)


def draw_dt_raw(key, part):
    key = jax.random.fold_in(key, 23)
    jitter_key, plateau_key, spike_key = jax.random.split(key, 3)
    jitter_values = jnp.clip(jax.random.normal(jitter_key, (HEADS, ROLLOUT_TOKENS), jnp.float32) * 0.6, -2.4, 2.4)
    plateau_values = jax.random.uniform(plateau_key, (HEADS, ROLLOUT_TOKENS // TOK_DEV), jnp.float32, -0.7, 0.7)
    plateau_values = jnp.repeat(plateau_values, TOK_DEV, axis=1)
    spike_positions = jax.random.randint(spike_key, (4,), 0, ROLLOUT_TOKENS)
    spike_values = jnp.zeros((ROLLOUT_TOKENS,), jnp.float32).at[spike_positions].set(1.0)
    return (jitter_values + plateau_values + spike_values[None, :] * math.log(0.35 * ROLLOUT_TOKENS)).astype(jnp.bfloat16)


def block_scale(own_key, extent, cuts, low, top_value):
    def one(axis_at, shards_of):
        steps = jax.random.uniform(jax.random.fold_in(jax.random.fold_in(own_key, 6), axis_at), (shards_of,), jnp.float32, low / len(cuts), top_value / len(cuts))
        return jnp.repeat(jnp.exp(steps), extent[axis_at] // shards_of).reshape((-1,) + (1,) * (len(extent) - axis_at - 1))

    gain = one(*cuts[0])
    for cut in cuts[1:]:
        gain = gain * one(*cut)
    return gain


def centred(own_key, extent, width, bound, cuts=(), held_as=jnp.bfloat16):
    factor_of = block_scale(own_key, extent, cuts, -0.22, 0.18) if cuts else 1.0
    values = jax.random.normal(own_key, extent, jnp.float32) * width * factor_of
    return jnp.minimum(jnp.maximum(values, -bound), bound).astype(held_as)


def setup_inputs(seed: int = 0, part: int = 0) -> dict:
    streams_of = jax.random.split(jax.random.key(seed), 12)
    part_keys = jax.random.split(jax.random.fold_in(streams_of[11], part), 12)
    x_raw = centred(part_keys[0], (ROLLOUT_TOKENS, HEADS * HEAD_DIM), 1.0, 6.0, ((0, 16), (1, 8)))
    b_raw = centred(part_keys[1], (ROLLOUT_TOKENS, GROUPS * STATE), 1.0, 6.0, ((0, 16), (1, 8)))
    c_raw = centred(part_keys[2], (ROLLOUT_TOKENS, GROUPS * STATE), 1.0, 6.0, ((0, 16), (1, 8)))
    dt_raw = draw_dt_raw(jax.random.fold_in(jax.random.fold_in(streams_of[11], part), 71), part)
    dt_bias = jnp.clip(-8.0 + 1.0 * jax.random.uniform(streams_of[4], (HEADS,), jnp.float32) ** block_scale(streams_of[4], (HEADS,), ((0, 8),), -0.2, 0.2), -8.0, -7.0)
    a_log = draw_a_log(jax.random.fold_in(streams_of[11], 71), part)
    skip_gain = jnp.clip(0.5 + 1.0 * jax.random.uniform(streams_of[6], (HEADS,), jnp.float32) ** block_scale(streams_of[6], (HEADS,), ((0, 8),), -0.2, 0.2), 0.5, 1.5)
    conv_x = centred(streams_of[7], (CONV, HEADS * HEAD_DIM), 0.5, 2.0, ((1, 8),), jnp.float32)
    conv_b = centred(streams_of[8], (CONV, GROUPS * STATE), 0.5, 2.0, ((1, 8),), jnp.float32)
    conv_c = centred(streams_of[9], (CONV, GROUPS * STATE), 0.5, 2.0, ((1, 8),), jnp.float32)
    grad_y = centred(part_keys[10], (ROLLOUT_TOKENS, HEADS * HEAD_DIM), 1.0, 6.0, ((0, 16), (1, 8)))
    return dict(x_raw=x_raw, b_raw=b_raw, c_raw=c_raw, dt_raw=dt_raw, dt_bias=dt_bias, a_log=a_log, skip_gain=skip_gain, conv_x=conv_x, conv_b=conv_b, conv_c=conv_c, grad_y=grad_y)


precise = lax.Precision.HIGHEST

def conv_silu(padded, taps):
    length = padded.shape[0] - taps.shape[0] + 1
    total = padded[0:length] * taps[0]
    for offset in range(1, taps.shape[0]):
        total = total + padded[offset:offset + length] * taps[offset]
    return jax.nn.silu(total)

def span_step(running, inputs):
    x_block, b_block, c_block, a_block, dt_block = inputs
    block_size = a_block.shape[1]
    head_count = x_block.shape[1]
    head_size = x_block.shape[2]
    group_count = b_block.shape[1]
    per_group = head_count // group_count
    state_size = b_block.shape[2]
    cumulative = jnp.cumsum(a_block, axis=1)
    position = jnp.arange(block_size)
    causal = position[:, None] >= position[None, :]
    exponent = jnp.where(causal[None], cumulative[:, :, None] - cumulative[:, None, :], 0.0)
    decay = jnp.where(causal[None], jnp.exp(exponent), 0.0)
    scores = jnp.einsum('ign,jgn->gij', c_block, b_block, precision=precise)
    mixing = scores[:, None] * decay.reshape(group_count, per_group, block_size, block_size) * dt_block.reshape(group_count, per_group, 1, block_size)
    x_group = x_block.reshape(block_size, group_count, per_group, head_size)
    inside = jnp.einsum('gkij,jgkp->igkp', mixing, x_group, precision=precise).reshape(block_size, head_count, head_size)
    state_group = running.reshape(group_count, per_group, head_size, state_size)
    entering = jnp.einsum('ign,gkpn->igkp', c_block, state_group, precision=precise).reshape(block_size, head_count, head_size)
    entering = entering * jnp.exp(cumulative).T[:, :, None]
    to_end = jnp.exp(cumulative[:, -1:] - cumulative) * dt_block
    written = jnp.einsum('jgkp,gkj,jgn->gkpn', x_group, to_end.reshape(group_count, per_group, block_size), b_block, precision=precise)
    written = written.reshape(head_count, head_size, state_size)
    return (jnp.exp(cumulative[:, -1])[:, None, None] * running + written, inside + entering)

def spanned(x_heads, b_conv, c_conv, log_decay, step_size, running):
    length = x_heads.shape[0]
    blocks = length // SPAN
    head_count = x_heads.shape[1]
    group_count = b_conv.shape[1] // STATE
    x_blocks = x_heads.reshape(blocks, SPAN, head_count, x_heads.shape[2])
    b_blocks = b_conv.reshape(blocks, SPAN, group_count, STATE)
    c_blocks = c_conv.reshape(blocks, SPAN, group_count, STATE)
    a_blocks = log_decay.reshape(head_count, blocks, SPAN).transpose(1, 0, 2)
    dt_blocks = step_size.reshape(head_count, blocks, SPAN).transpose(1, 0, 2)
    final_state, outputs = lax.scan(jax.checkpoint(span_step), running, (x_blocks, b_blocks, c_blocks, a_blocks, dt_blocks))
    return (outputs.reshape(length, head_count, x_heads.shape[2]), final_state)

def forward(x_float, b_float, c_float, dt_float, dt_bias, a_log, skip_gain, conv_x, conv_b, conv_c):
    margin = conv_x.shape[0] - 1
    x_conv = conv_silu(jnp.pad(x_float, ((margin, 0), (0, 0))), conv_x)
    b_conv = conv_silu(jnp.pad(b_float, ((margin, 0), (0, 0))), conv_b)
    c_conv = conv_silu(jnp.pad(c_float, ((margin, 0), (0, 0))), conv_c)
    step_size = jax.nn.softplus(dt_float + dt_bias[:, None])
    log_decay = -jnp.exp(a_log)[:, None] * step_size
    length = x_conv.shape[0]
    x_heads = x_conv.reshape(length, HEADS, HEAD_DIM)
    start_state = jnp.zeros((HEADS, HEAD_DIM, STATE), jnp.float32)
    y_heads, final_state = spanned(x_heads, b_conv, c_conv, log_decay, step_size, start_state)
    y_heads = y_heads + skip_gain[None, :, None] * x_heads
    return y_heads.reshape(length, HEADS * HEAD_DIM)

def reference(x_raw, b_raw, c_raw, dt_raw, dt_bias, a_log, skip_gain, conv_x, conv_b, conv_c, grad_y):

    def scan_layer(x_float, b_float, c_float, dt_float):
        return forward(x_float, b_float, c_float, dt_float, dt_bias, a_log, skip_gain, conv_x, conv_b, conv_c)
    y_out, pullback = jax.vjp(scan_layer, x_raw.astype(jnp.float32), b_raw.astype(jnp.float32), c_raw.astype(jnp.float32), dt_raw.astype(jnp.float32))
    grad_x, grad_b, grad_c, grad_dt = pullback(grad_y.astype(jnp.float32))
    return (y_out, grad_x, grad_b, grad_c, grad_dt)
```

```python
import functools

import jax
import jax.numpy as jnp
from jax import lax
from jax.experimental import pallas as pl
from jax.experimental.pallas import tpu as pltpu
from jax.sharding import PartitionSpec as P

f32 = jnp.float32
bf16 = jnp.bfloat16

TOKENS = 256
SUB = 128
HEADS = 16
HEAD_DIM = 64
STATE = 128
WIDTH = HEADS * HEAD_DIM
PAIRS = HEADS // 2
RIM = 3
RANKS = 16
CHUNK = 144
NEG = -1e30
CODE_SPAN = 200.0

NN = ((1,), (0,))
NT = ((1,), (1,))
TN = ((0,), (0,))


def dot(a, b, dims=NN):
    return lax.dot_general(a, b, (dims, ((), ())), preferred_element_type=f32)


def split2(v):
    hi = v.astype(bf16)
    return hi, (v - hi.astype(f32)).astype(bf16)


def split3(v):
    hi = v.astype(bf16)
    rest = v - hi.astype(f32)
    mid = rest.astype(bf16)
    return hi, mid, (rest - mid.astype(f32)).astype(bf16)


def dot3(a, b, dims=NN):
    return dot(a[0], b[0], dims) + dot(a[1], b[0], dims) + dot(a[0], b[1], dims)


def iota(shape, axis):
    return lax.broadcasted_iota(jnp.int32, shape, axis)


def onehot(mask):
    return jnp.where(mask, 1.0, 0.0).astype(bf16)


def to_column(row):
    n = row.shape[1]
    eye = iota((n, n), 0) == iota((n, n), 1)
    return jnp.sum(jnp.where(eye, row, 0.0), axis=1, keepdims=True)


def low_half(shape):
    return iota(shape, 1) < HEAD_DIM


def swap_halves(v):
    return pltpu.roll(v, HEAD_DIM, 1)


def encode(v):
    top = jnp.max(jnp.abs(v), axis=0, keepdims=True)
    scale = (jnp.maximum(top, 1e-30) * 1.01).astype(bf16).astype(f32)
    unit = jnp.abs(v) * (CODE_SPAN / scale)
    size = jnp.exp2(unit - CODE_SPAN / 2)
    return jnp.where(v < 0, -size, size).astype(bf16), scale


def decode(code, scale):
    v = code.astype(f32)
    unit = jnp.log2(jnp.abs(v)) + CODE_SPAN / 2
    size = unit * (scale * (1.0 / CODE_SPAN))
    return jnp.where(v < 0, -size, size)


def split_heads(pair):
    top, bottom = pair[:HEAD_DIM], pair[HEAD_DIM:]
    low = low_half(top.shape)
    return (
        jnp.where(low, top, swap_halves(bottom)),
        jnp.where(low, swap_halves(top), bottom),
    )


def join_heads(first, second):
    low = low_half(first.shape)
    return (
        jnp.where(low, first, swap_halves(second)),
        jnp.where(low, swap_halves(first), second),
    )


def transpose_rows(arrays):
    rows = sum(a.shape[0] for a in arrays)
    pad = jnp.zeros((128 - rows, TOKENS), f32)
    return split3(jnp.concatenate(list(arrays) + [pad], axis=0).T)


def spread(parts, which, first_head, lanes_per_head, lanes):
    shape = (128, lanes)
    hot = onehot(iota(shape, 0) == which * HEADS + first_head + iota(shape, 1) // lanes_per_head)
    return dot(parts[0], hot) + dot(parts[1], hot) + dot(parts[2], hot)


def decay_terms(cum, step):
    first = iota(cum.shape, 1) < SUB
    end0 = cum[:, SUB - 1 : SUB]
    end1 = cum[:, TOKENS - 1 : TOKENS]
    inner = jnp.exp(cum)
    outer = jnp.exp(jnp.where(first, end0, end1) - cum) * step
    from_start = jnp.where(first, inner, inner * jnp.exp(end0))
    to_end = jnp.where(first, outer * jnp.exp(end1), outer)
    return inner, outer, from_start, to_end, end0 + end1


def enter_kernel(
    x_raw, b_raw, c_raw, before, dt_raw, dt_bias, a_log, conv_x, conv_b, conv_c, grad_y,
    pay, x_out, slope_out, bc_out, slope_bc_out, cum_out, step_out,
    rows_scr,
):
    pre = dt_raw[...].astype(f32) + to_column(dt_bias[...])
    step = jnp.maximum(pre, 0.0) + jnp.log1p(jnp.exp(-jnp.abs(pre)))
    log_decay = -jnp.exp(to_column(a_log[...])) * step
    r, c = iota((TOKENS, TOKENS), 0), iota((TOKENS, TOKENS), 1)
    upto = onehot((r <= c) & (r // SUB == c // SUB))
    parts = split3(log_decay)
    cum = dot(parts[2], upto) + dot(parts[1], upto) + dot(parts[0], upto)
    cum_out[...] = cum
    step_out[...] = step
    _, _, from_start, to_end, total = decay_terms(cum, step)
    columns = transpose_rows([from_start, to_end])

    def conv(raw, halo, taps, lanes):
        rows_scr[8 - RIM : 8, lanes] = halo.astype(f32)
        rows_scr[8:, lanes] = raw.astype(f32)
        v = taps[0:1] * rows_scr[8 - RIM : 8 - RIM + TOKENS, lanes]
        for k in range(1, RIM + 1):
            v += taps[k : k + 1] * rows_scr[8 - RIM + k : 8 - RIM + k + TOKENS, lanes]
        gate = 1.0 / (1.0 + jnp.exp(-v))
        return v * gate, gate * (1.0 + v * (1.0 - gate))

    b, slope_b = conv(b_raw[...], before[:, WIDTH : WIDTH + STATE], conv_b[...], pl.ds(0, 128))
    c, slope_c = conv(c_raw[...], before[:, WIDTH + STATE :], conv_c[...], pl.ds(0, 128))
    bc_out[:, :STATE] = b
    bc_out[:, STATE:] = c
    slope_bc_out[:, :STATE] = slope_b
    slope_bc_out[:, STATE:] = slope_c
    bt = split2(b.T)
    ct = split2(c.T)
    for pair in range(PAIRS):
        lanes = pl.ds(pair * 128, 128)
        x, slope = conv(x_raw[:, lanes], before[:, pair * 128 : pair * 128 + 128], conv_x[:, lanes], lanes)
        x_out[:, lanes] = x
        slope_out[:, lanes] = slope
        xw = x * spread(columns, 1, 2 * pair, HEAD_DIM, 128)
        ge = grad_y[:, lanes].astype(f32) * spread(columns, 0, 2 * pair, HEAD_DIM, 128)
        s_heads = split_heads(dot3(bt, split2(xw)))
        g_heads = split_heads(dot3(ct, split2(ge)))
        for k in range(2):
            head = 2 * pair + k
            s_code, s_scale = encode(s_heads[k])
            g_code, g_scale = encode(g_heads[k])
            pay[head, 0:64, :] = s_code
            pay[head, 64:128, :] = g_code
            d = split3(jnp.broadcast_to(total[head : head + 1], (1, 128)))
            at = iota((16, 128), 0)
            aux = jnp.where(at == 0, s_scale, g_scale)
            for n, part in enumerate(d):
                aux = jnp.where(at == 2 + n, part.astype(f32), aux)
            pay[head, 128:144, :] = aux.astype(bf16)


def scan_kernel(got, back):
    def aux_row(k, n):
        return got[k, 128:144, :].astype(f32)[n : n + 1]

    decay = [jnp.exp(aux_row(k, 2) + aux_row(k, 3) + aux_row(k, 4)) for k in range(RANKS)]
    scales = [[None, None] for _ in range(RANKS)]
    run = jnp.zeros((HEAD_DIM, 128), f32)
    for k in range(RANKS):
        code, scales[k][0] = encode(run)
        back[k, 0:64, :] = code
        if k < RANKS - 1:
            run = decay[k] * run + decode(got[k, 0:64, :], aux_row(k, 0))
    run = jnp.zeros((HEAD_DIM, 128), f32)
    for k in reversed(range(RANKS)):
        code, scales[k][1] = encode(run)
        back[k, 64:128, :] = code
        if k > 0:
            run = decay[k] * run + decode(got[k, 64:128, :], aux_row(k, 1))
    at = iota((16, 128), 0)
    for k in range(RANKS):
        back[k, 128:144, :] = jnp.where(at == 0, scales[k][0], scales[k][1]).astype(bf16)


def block_kernel(
    x_in, grad_y, bc_in, cum_in, step_in, skip,
    y_out, dx_out, dbc_out, sums_out,
    ds_scr, diag_scr, cols_scr, sc_scr, row_scr,
):
    cum, step = cum_in[...], step_in[...]
    shifted = cum - jnp.log(step)
    for head in range(HEADS):
        row_scr[head] = jnp.broadcast_to(cum[head : head + 1], (8, TOKENS))
        row_scr[HEADS + head] = jnp.broadcast_to(shifted[head : head + 1], (8, TOKENS))
    inner, outer, _, _, _ = decay_terms(cum, step)
    for n, part in enumerate(transpose_rows([cum, shifted, inner, outer, step])):
        cols_scr[n] = part
    b, c = bc_in[:, :STATE], bc_in[:, STATE:]
    r, l = iota((SUB, SUB), 0), iota((SUB, SUB), 1)
    b2, c2 = split2(b), split2(c)

    def rows(parts, s):
        return tuple(p[s * SUB : s * SUB + SUB] for p in parts)

    for s in range(2):
        sc_scr[s] = jnp.where(r > l, dot3(rows(c2, s), rows(b2, s), NT), 0.0)
        sc_scr[2 + s] = jnp.where(l > r, dot3(rows(b2, s), rows(c2, s), NT), 0.0)
    sc_scr[4] = dot3(rows(c2, 1), rows(b2, 0), NT)
    sc_scr[5] = dot3(rows(b2, 0), rows(c2, 1), NT)
    ds_scr[...] = jnp.zeros_like(ds_scr)
    sums_out[...] = jnp.zeros_like(sums_out)
    diag = jnp.broadcast_to(jnp.sum(b * c, axis=1, keepdims=True), (TOKENS, 128))
    diag_scr[0] = diag
    diag_scr[1] = jnp.zeros((TOKENS, 128), f32)
    low = low_half((SUB, 128))

    def pair_step(pair, carry):
        lanes = pl.ds(pl.multiple_of(pair * 128, 128), 128)
        cols = (cols_scr[0], cols_scr[1], cols_scr[2])
        x = x_in[:, lanes]
        g = grad_y[:, lanes]
        gf = g.astype(f32)
        xh, xl = split2(x)
        cum_cols = spread(cols, 0, 2 * pair, 128, 256)
        shifted_cols = spread(cols, 1, 2 * pair, 128, 256)
        inner_x = spread(cols, 2, 2 * pair, HEAD_DIM, 128)
        outer_x = spread(cols, 3, 2 * pair, HEAD_DIM, 128)
        step_x = spread(cols, 4, 2 * pair, HEAD_DIM, 128)
        ys, dxs = [], []
        for s in range(2):
            at = slice(s * SUB, s * SUB + SUB)
            xh_s, xl_s, g_s = xh[at], xl[at], g[at]
            xh2 = jnp.concatenate([xh_s, xh_s], axis=0)
            g2 = jnp.concatenate([g_s, g_s], axis=0)
            xhl = jnp.concatenate([xh_s, xl_s], axis=1)
            y_k, dx_k = [], []
            for k in range(2):
                head = 2 * pair + k
                row_cum = row_scr[head][0:1, at]
                row_shift = row_scr[HEADS + head][0:1, at]
                col_cum = cum_cols[at, k * 128 : k * 128 + 128]
                col_shift = shifted_cols[at, k * 128 : k * 128 + 128]
                decay = jnp.exp(jnp.where(r > l, col_cum - row_shift, NEG))
                decay_t = jnp.exp(jnp.where(l > r, row_cum - col_shift, NEG))
                mh, ml = split2(sc_scr[s] * decay)
                th, tl = split2(sc_scr[2 + s] * decay_t)
                y_k.append(dot(jnp.concatenate([mh, ml], axis=1), xh2) + dot(mh, xl_s))
                dx_k.append(dot(jnp.concatenate([th, tl], axis=1), g2))
                g_k = jnp.where(low if k == 0 else ~low, g_s.astype(f32), 0.0).astype(bf16)
                dm = dot(jnp.concatenate([g_k, g_k], axis=1), xhl, NT)
                ds_scr[s] += dm * decay
            ys.append(jnp.where(low, y_k[0], y_k[1]))
            dxs.append(jnp.where(low, dx_k[0], dx_k[1]))
        xw = split2(x[:SUB] * outer_x[:SUB])
        ge = split2(gf[SUB:] * inner_x[SUB:])
        ys[1] += inner_x[SUB:] * dot3(split2(sc_scr[4]), xw)
        dxs[0] += outer_x[:SUB] * dot3(split2(sc_scr[5]), ge)
        ds_scr[2] += dot3(ge, xw, NT)
        y = jnp.concatenate(ys, axis=0)
        dx = jnp.concatenate(dxs, axis=0)
        xg = x * gf
        xdx = x * dx
        hot = onehot(iota((HEADS, 128), 0) == 2 * pair + iota((HEADS, 128), 1) // HEAD_DIM)

        def head_sums(v):
            hi, mid, lo = split3(v)
            return dot(hot, hi, NT) + dot(hot, mid, NT) + dot(hot, lo, NT)

        sums_out[0] += head_sums(gf * y - xdx)
        sums_out[1] += head_sums(xdx)
        sums_out[2] += head_sums(xg)
        diag_scr[1] += step_x * xg
        low2 = low_half((TOKENS, 128))
        direct = jnp.where(low2, skip[0, 2 * pair], skip[0, 2 * pair + 1]) + diag_scr[0] * step_x
        y_out[:, lanes] = y + direct * x
        dx_out[:, lanes] = dx + direct * gf
        return carry

    lax.fori_loop(0, PAIRS, pair_step, 0)
    d_diag = jnp.sum(diag_scr[1], axis=1, keepdims=True)
    db = d_diag * c
    dc = d_diag * b
    for s in range(2):
        d2 = split2(jnp.where(r > l, ds_scr[s], 0.0))
        t2 = split2(jnp.where(r > l, ds_scr[s], 0.0).T)
        at = slice(s * SUB, s * SUB + SUB)
        dc_s = dc[at] + dot3(d2, rows(b2, s))
        db_s = db[at] + dot3(t2, rows(c2, s))
        if s == 0:
            db_s += dot3(split2(ds_scr[2].T), rows(c2, 1))
        else:
            dc_s += dot3(split2(ds_scr[2]), rows(b2, 0))
        dbc_out[at, :STATE] = db_s
        dbc_out[at, STATE:] = dc_s
    ones = onehot(iota((16, 128), 0) >= 0)
    bc = split3(b * c)
    diag_row = dot(ones, bc[0], NT) + dot(ones, bc[1], NT) + dot(ones, bc[2], NT)
    sums_out[1] = sums_out[1] / step + diag_row * sums_out[2]


def leave_kernel(
    back, x_in, grad_y, bc_in, slope_in, slope_bc_in, cum_in, step_in, y_in, dx_in, dbc_in, sums_in,
    dt_raw, dt_bias, a_log,
    y_out, dpre_out, dpre_bc_out, dt_out,
    e_scr, f_scr,
):
    cum, step = cum_in[...], step_in[...]
    _, _, from_start, to_end, total = decay_terms(cum, step)
    columns = transpose_rows([from_start, to_end])
    b2, c2 = split2(bc_in[:, :STATE]), split2(bc_in[:, STATE:])
    db = dbc_in[:, :STATE]
    dc = dbc_in[:, STATE:]
    carried = jnp.zeros((HEADS, TOKENS), f32)
    later = jnp.zeros((HEADS, TOKENS), f32)
    both = jnp.zeros((HEADS, 8), f32)
    for pair in range(PAIRS):
        lanes = pl.ds(pair * 128, 128)
        codes = []
        for k in range(2):
            head = 2 * pair + k
            aux = back[head, 128:144, :].astype(f32)
            codes.append((decode(back[head, 0:64, :], aux[0:1]), decode(back[head, 64:128, :], aux[1:2])))
        e = jnp.concatenate(join_heads(codes[0][0], codes[1][0]), axis=0)
        f = jnp.concatenate(join_heads(codes[0][1], codes[1][1]), axis=0)
        e2, f2 = split2(e), split2(f)
        start_x = spread(columns, 0, 2 * pair, HEAD_DIM, 128)
        end_x = spread(columns, 1, 2 * pair, HEAD_DIM, 128)
        ge = grad_y[:, lanes].astype(f32) * start_x
        xw = x_in[:, lanes] * end_x
        ce = dot3(c2, e2)
        bf = dot3(b2, f2)
        y_out[:, lanes] = y_in[:, lanes] + start_x * ce
        dpre_out[:, lanes] = (dx_in[:, lanes] + end_x * bf) * slope_in[:, lanes]
        dc += dot3(split2(ge), e2, NT)
        db += dot3(split2(xw), f2, NT)
        hot = onehot(iota((HEADS, 128), 0) == 2 * pair + iota((HEADS, 128), 1) // HEAD_DIM)

        def head_sums(v):
            hi, mid, lo = split3(v)
            return dot(hot, hi, NT) + dot(hot, mid, NT) + dot(hot, lo, NT)

        carried += head_sums(ge * ce)
        later += head_sums(xw * bf)
        both += head_sums(jnp.broadcast_to(jnp.sum(e * f, axis=0, keepdims=True), (8, 128)))
    dpre_bc_out[:, :STATE] = db * slope_bc_in[:, :STATE]
    dpre_bc_out[:, STATE:] = dc * slope_bc_in[:, STATE:]
    r, c = iota((TOKENS, TOKENS), 0), iota((TOKENS, TOKENS), 1)
    suffix = onehot(r >= c)
    prefix = onehot(r < c)

    def summed(v, tri):
        hi, mid, lo = split3(v)
        return dot(lo, tri) + dot(mid, tri) + dot(hi, tri)

    d_decay = summed(sums_in[0] + carried, suffix) + summed(later, prefix) + jnp.exp(total) * both[:, 0:1]
    d_step = sums_in[1] + later / step - jnp.exp(to_column(a_log[...])) * d_decay
    pre = dt_raw[...].astype(f32) + to_column(dt_bias[...])
    dt_out[...] = d_step / (1.0 + jnp.exp(-pre))


def settle_kernel(dpre, dpre_bc, after, conv_x, conv_b, conv_c, gx, gb, gc, rows_scr):
    def unconv(d, halo, taps, lanes):
        rows_scr[0:TOKENS, lanes] = d
        rows_scr[TOKENS : TOKENS + RIM, lanes] = halo
        v = taps[RIM : RIM + 1] * d
        for k in range(RIM):
            v += taps[k : k + 1] * rows_scr[RIM - k : RIM - k + TOKENS, lanes]
        return v

    for pair in range(PAIRS):
        lanes = pl.ds(pair * 128, 128)
        gx[:, lanes] = unconv(dpre[:, lanes], after[:, pair * 128 : pair * 128 + 128], conv_x[:, lanes], lanes)
    gb[...] = unconv(dpre_bc[:, :STATE], after[:, WIDTH : WIDTH + STATE], conv_b[...], pl.ds(0, 128))
    gc[...] = unconv(dpre_bc[:, STATE:], after[:, WIDTH + STATE :], conv_c[...], pl.ds(0, 128))


VMEM = pl.BlockSpec(memory_space=pltpu.VMEM)
SMEM = pl.BlockSpec(memory_space=pltpu.SMEM)
PARAMS = pltpu.CompilerParams(vmem_limit_bytes=48 * 1024 * 1024)


def call(kernel, outs, ins, scratch=(), flops=0, specs=None):
    shapes = [jax.ShapeDtypeStruct(s, d) for s, d in outs]
    moved = sum(a.size * a.dtype.itemsize for a in ins) + sum(
        s.size * s.dtype.itemsize for s in shapes
    )
    return pl.pallas_call(
        kernel,
        out_shape=shapes,
        in_specs=specs or [VMEM] * len(ins),
        out_specs=[VMEM] * len(outs),
        scratch_shapes=list(scratch),
        compiler_params=PARAMS,
        cost_estimate=pl.CostEstimate(flops=flops, bytes_accessed=moved, transcendentals=0),
    )(*ins)


def on_device(
    x_raw, b_raw, c_raw, dt_raw, dt_bias, a_log, skip_gain, conv_x, conv_b, conv_c, grad_y
):
    wide, slim, bc = (TOKENS, WIDTH), (HEADS, TOKENS), (TOKENS, 2 * STATE)
    dt_bias, a_log, skip_gain = (v.reshape(1, HEADS) for v in (dt_bias, a_log, skip_gain))
    edge = jnp.concatenate([v[TOKENS - RIM :] for v in (x_raw, b_raw, c_raw)], axis=1)
    before = lax.ppermute(edge, "context", [(i, i + 1) for i in range(RANKS - 1)])
    pay, x, slope, bcs, slope_bc, cum, step = call(
        enter_kernel,
        [((HEADS, CHUNK, 128), bf16), (wide, f32), (wide, f32), (bc, f32), (bc, f32), (slim, f32), (slim, f32)],
        [x_raw, b_raw, c_raw, before, dt_raw, dt_bias, a_log, conv_x, conv_b, conv_c, grad_y],
        [pltpu.VMEM((TOKENS + 8, WIDTH), f32)],
        flops=2_000_000_000,
    )
    got = lax.all_to_all(pay, "context", 0, 0, tiled=True)
    y_part, dx_part, dbc_part, sums = call(
        block_kernel,
        [(wide, f32), (wide, f32), (bc, f32), ((3,) + slim, f32)],
        [x, grad_y, bcs, cum, step, skip_gain],
        [
            pltpu.VMEM((3, SUB, SUB), f32),
            pltpu.VMEM((2, TOKENS, 128), f32),
            pltpu.VMEM((3, TOKENS, 128), bf16),
            pltpu.VMEM((6, SUB, SUB), f32),
            pltpu.VMEM((2 * HEADS, 8, TOKENS), f32),
        ],
        flops=8_000_000_000,
        specs=[VMEM] * 5 + [SMEM],
    )
    (answer,) = call(scan_kernel, [((RANKS, CHUNK, 128), bf16)], [got])
    back = lax.all_to_all(answer, "context", 0, 0, tiled=True)
    y_out, dpre, dpre_bc, grad_dt = call(
        leave_kernel,
        [(wide, f32), (wide, f32), (bc, f32), (slim, f32)],
        [back, x, grad_y, bcs, slope, slope_bc, cum, step, y_part, dx_part, dbc_part, sums, dt_raw, dt_bias, a_log],
        [pltpu.VMEM((8, 128), f32), pltpu.VMEM((8, 128), f32)],
        flops=2_000_000_000,
    )
    rim = jnp.concatenate([dpre[:RIM], dpre_bc[:RIM]], axis=1)
    after = lax.ppermute(rim, "context", [(i, i - 1) for i in range(1, RANKS)])
    grad_x, grad_b, grad_c = call(
        settle_kernel,
        [(wide, f32), ((TOKENS, STATE), f32), ((TOKENS, STATE), f32)],
        [dpre, dpre_bc, after, conv_x, conv_b, conv_c],
        [pltpu.VMEM((TOKENS + 8, WIDTH), f32)],
        flops=2_000_000,
    )
    return (y_out, grad_x, grad_b, grad_c, grad_dt)


def solution(mesh):
    tokens = P(("dp", "context"), "tensor")
    heads = P("tensor", ("dp", "context"))
    one, taps = P("tensor"), P(None, "tensor")
    return jax.shard_map(
        on_device,
        mesh=mesh,
        in_specs=(tokens, tokens, tokens, heads, one, one, one, taps, taps, taps, tokens),
        out_specs=(tokens, tokens, tokens, tokens, heads),
        check_vma=False,
    )
```

```python
import functools

import jax
import jax.numpy as jnp
from jax import lax
from jax.experimental import pallas as pl
from jax.experimental.pallas import tpu as pltpu
from jax.sharding import PartitionSpec as P

f32 = jnp.float32
bf16 = jnp.bfloat16

TOKENS = 256
SUB = 128
HEADS = 16
HEAD_DIM = 64
STATE = 128
WIDTH = HEADS * HEAD_DIM
PAIRS = HEADS // 2
RIM = 3
RANKS = 16
SIDE = 4
QUARTER = HEADS // SIDE
ROWMSG = 80
CHUNK = 144
ALL = WIDTH + 2 * STATE
PART = 256
PARTS = WIDTH // PART
NEG = -1e30
CODE_SPAN = 248.0

NN = ((1,), (0,))
NT = ((1,), (1,))
TN = ((0,), (0,))


def dot(a, b, dims=NN):
    return lax.dot_general(a, b, (dims, ((), ())), preferred_element_type=f32)


def split2(v):
    hi = v.astype(bf16)
    return hi, (v - hi.astype(f32)).astype(bf16)


def split3(v):
    hi = v.astype(bf16)
    rest = v - hi.astype(f32)
    mid = rest.astype(bf16)
    return hi, mid, (rest - mid.astype(f32)).astype(bf16)


def dot3(a, b, dims=NN):
    return dot(a[0], b[0], dims) + dot(a[1], b[0], dims) + dot(a[0], b[1], dims)


def iota(shape, axis):
    return lax.broadcasted_iota(jnp.int32, shape, axis)


def onehot(mask):
    return jnp.where(mask, 1.0, 0.0).astype(bf16)


def to_column(row):
    n = row.shape[1]
    eye = iota((n, n), 0) == iota((n, n), 1)
    return jnp.sum(jnp.where(eye, row, 0.0), axis=1, keepdims=True)


def low_half(shape):
    return iota(shape, 1) < HEAD_DIM


def swap_halves(v):
    return pltpu.roll(v, HEAD_DIM, 1)


def encode(v):
    top = jnp.max(jnp.abs(v), axis=0, keepdims=True)
    scale = (jnp.maximum(top, 1e-30) * 1.01).astype(bf16).astype(f32)
    unit = jnp.abs(v) * (CODE_SPAN / scale)
    size = jnp.exp2(unit - CODE_SPAN / 2)
    return jnp.where(v < 0, -size, size).astype(bf16), scale


def decode(code, scale):
    v = code.astype(f32)
    unit = jnp.log2(jnp.abs(v)) + CODE_SPAN / 2
    size = unit * (scale * (1.0 / CODE_SPAN))
    return jnp.where(v < 0, -size, size)


def split_heads(pair):
    top, bottom = pair[:HEAD_DIM], pair[HEAD_DIM:]
    low = low_half(top.shape)
    return (
        jnp.where(low, top, swap_halves(bottom)),
        jnp.where(low, swap_halves(top), bottom),
    )


def join_heads(first, second):
    low = low_half(first.shape)
    return (
        jnp.where(low, first, swap_halves(second)),
        jnp.where(low, swap_halves(first), second),
    )


def stack_columns(arrays):
    stacked = jnp.concatenate(list(arrays), axis=0)
    parts = [p.astype(f32) for p in split3(stacked)]
    rows = 3 * stacked.shape[0]
    full = 128 if rows <= 128 else 256
    parts.append(jnp.zeros((full - rows, TOKENS), f32))
    return jnp.concatenate(parts, axis=0).T.astype(bf16)


def spread_matrix(count, full, which, first_head, lanes_per_head, lanes):
    r, l = iota((full, lanes), 0), iota((full, lanes), 1)
    rows = r - (r // (count * HEADS)) * (count * HEADS)
    return onehot((r < 3 * count * HEADS) & (rows - l // lanes_per_head == which * HEADS + first_head))


def sum_matrix(rows, offset):
    r, l = iota((rows, 128), 0), iota((rows, 128), 1)
    return onehot(r // HEAD_DIM + offset == l)


def decay_terms(cum, step):
    first = iota(cum.shape, 1) < SUB
    end0 = cum[:, SUB - 1 : SUB]
    end1 = cum[:, TOKENS - 1 : TOKENS]
    inner = jnp.exp(cum)
    outer = jnp.exp(jnp.where(first, end0, end1) - cum) * step
    from_start = jnp.where(first, inner, inner * jnp.exp(end0))
    to_end = jnp.where(first, outer * jnp.exp(end1), outer)
    return inner, outer, from_start, to_end, end0 + end1


def begin(moves, sems):
    copies = [pltpu.make_async_copy(a, b, sems.at[n]) for n, (a, b) in enumerate(moves)]
    for copy in copies:
        copy.start()
    return copies


def wait(copies):
    for copy in copies:
        copy.wait()


def part(n):
    return pl.ds(n * PART, PART)


def silu_of(v):
    return v / (1.0 + jnp.exp(-v))


def slope_of(v):
    gate = 1.0 / (1.0 + jnp.exp(-v))
    return v * gate, gate * (1.0 + v * (1.0 - gate))


def conv_rows(rows_scr, taps, lanes):
    v = taps[0:1] * rows_scr[8 - RIM : 8 - RIM + TOKENS, lanes]
    for k in range(1, RIM + 1):
        v += taps[k : k + 1] * rows_scr[8 - RIM + k : 8 - RIM + k + TOKENS, lanes]
    return v


B_LANES = pl.ds(WIDTH, STATE)
C_LANES = pl.ds(WIDTH + STATE, STATE)


def edge_kernel(x_raw, b_raw, c_raw, edge, scr, sems):
    rows = pl.ds(TOKENS - 16, 16)
    wait(
        begin(
            [
                (x_raw.at[rows, :], scr.at[:, pl.ds(0, WIDTH)]),
                (b_raw.at[rows, :], scr.at[:, B_LANES]),
                (c_raw.at[rows, :], scr.at[:, C_LANES]),
            ],
            sems,
        )
    )
    edge[...] = scr[...].astype(f32)[16 - RIM :].astype(bf16)


def first_kernel(
    xs, gs, bs, cs, dts, bias, rate, taps_x, taps_b, taps_c,
    sg, pre16, end16, ge16, taps_out, total_out, cum_out, step_out, columns_out,
    rows_scr,
):
    pre = dts[...].astype(f32) + to_column(bias[...])
    step = jnp.maximum(pre, 0.0) + jnp.log1p(jnp.exp(-jnp.abs(pre)))
    log_decay = -jnp.exp(to_column(rate[...])) * step
    r, c = iota((TOKENS, TOKENS), 0), iota((TOKENS, TOKENS), 1)
    upto = onehot((r <= c) & (r // SUB == c // SUB))
    parts = split3(log_decay)
    cum = dot(parts[2], upto) + dot(parts[1], upto) + dot(parts[0], upto)
    cum_out[...] = cum
    step_out[...] = step
    _, _, from_start, to_end, total = decay_terms(cum, step)
    for head in range(HEADS):
        total_out[head] = jnp.broadcast_to(total[head : head + 1], (8, 128))
    columns = stack_columns([from_start, to_end])
    columns_out[...] = columns
    taps_out[:, 0:WIDTH] = taps_x[...]
    taps_out[:, WIDTH : WIDTH + STATE] = taps_b[...]
    taps_out[:, WIDTH + STATE :] = taps_c[...]
    rows_scr[0:8, :] = jnp.zeros((8, ALL), f32)
    known = iota((TOKENS, 128), 0) >= 16
    turned = []
    for raw, taps, lanes in ((bs, taps_b, B_LANES), (cs, taps_c, C_LANES)):
        rows_scr[8:, lanes] = raw[...].astype(f32)
        v = conv_rows(rows_scr, taps[...], lanes)
        pre16[:, lanes] = v[:16]
        turned.append(split2(jnp.where(known, silu_of(v), 0.0).T))
    bt, ct = turned
    for n in range(PARTS):
        lanes = part(n)
        heads = n * PART // HEAD_DIM
        start_x = dot(columns, spread_matrix(2, 128, 0, heads, HEAD_DIM, PART))
        end_x = dot(columns, spread_matrix(2, 128, 1, heads, HEAD_DIM, PART))
        rows_scr[8:, lanes] = xs[:, lanes].astype(f32)
        v = conv_rows(rows_scr, taps_x[:, lanes], lanes)
        pre16[:, lanes] = v[:16]
        end16[:, lanes] = end_x[:16]
        xw = silu_of(v) * end_x
        ge = gs[:, lanes].astype(f32) * start_x
        ge16[:, lanes] = ge[:16]
        sg[0, :, lanes] = dot3(bt, split2(xw))
        sg[1, :, lanes] = dot3(ct, split2(ge))


def quarter(q):
    return pl.ds(pl.multiple_of(q * PART, PART), PART)


def place():
    here = lax.axis_index("context")
    return lax.rem(here, SIDE), lax.div(here, SIDE)


def write_aux(scales, total):
    at = iota((16, 128), 0)
    aux = jnp.where(at == 0, scales[0], scales[-1])
    for m, piece in enumerate(split3(total)):
        aux = jnp.where(at == 2 + m, piece.astype(f32), aux)
    return aux.astype(bf16)


def send_kernel(before, sg, pre16, end16, ge16, taps, total, *refs):
    pays, (xw_scr, ge_scr) = refs[:SIDE], refs[SIDE:]
    halo = before[...].astype(f32)
    v = pre16[...]
    at = iota((16, ALL), 0)
    for row in range(RIM):
        more = taps[0:1] * halo[row : row + 1]
        for k in range(1, RIM - row):
            more += taps[k : k + 1] * halo[row + k : row + k + 1]
        v += jnp.where(at == row, more, 0.0)
    act = silu_of(v)
    xw_scr[...] = act[:, :WIDTH] * end16[...]
    ge_scr[...] = ge16[...]
    b = split2(act[:, WIDTH : WIDTH + STATE])
    c = split2(act[:, WIDTH + STATE :])
    x, _ = place()
    for shift, pay in enumerate(pays):
        q = lax.rem(x + shift, SIDE)
        lanes = quarter(q)
        s = sg[0, :, lanes] + dot3(b, split2(xw_scr[:, lanes]), TN)
        g = sg[1, :, lanes] + dot3(c, split2(ge_scr[:, lanes]), TN)
        for half in range(PART // 128):
            s_heads = split_heads(s[:, half * 128 : half * 128 + 128])
            g_heads = split_heads(g[:, half * 128 : half * 128 + 128])
            for k in range(2):
                slot = 2 * half + k
                s_code, s_scale = encode(s_heads[k])
                g_code, g_scale = encode(g_heads[k])
                pay[slot, 0:64, :] = s_code
                pay[slot, 64:128, :] = g_code
                pay[slot, 128:144, :] = write_aux((s_scale, g_scale), total[q * QUARTER + slot][0:1])


def row_kernel(*refs):
    pays, tick, refs = refs[:SIDE], refs[SIDE], refs[SIDE + 1 :]
    (*sends, s_out, g_out, d_out) = refs
    x, y = place()
    for shift, pay in enumerate(pays):
        source = lax.rem(x - shift + SIDE, SIDE)
        for k in range(QUARTER):
            aux = pay[k, 128:144, :].astype(f32)
            s_out[source, k] = decode(pay[k, 0:64, :], aux[0:1])
            g_out[source, k] = decode(pay[k, 64:128, :], aux[1:2])
            d_out[source, k] = jnp.broadcast_to(aux[2:3] + aux[3:4] + aux[4:5], (8, 128))
    for k in range(QUARTER):
        s_run, g_run = s_out[0, k], g_out[SIDE - 1, k]
        for n in range(1, SIDE):
            s_run = jnp.exp(d_out[n, k][0:1]) * s_run + s_out[n, k]
            m = SIDE - 1 - n
            g_run = jnp.exp(d_out[m, k][0:1]) * g_run + g_out[m, k]
        total = sum(d_out[n, k][0:1] for n in range(SIDE))
        for shift, message in enumerate(sends, 1):
            code, scale = encode(jnp.where(y + shift < SIDE, s_run, g_run))
            message[k, 0:64, :] = code
            message[k, 64:80, :] = write_aux((scale,), total)


def column_kernel(*refs):
    rows, (s_in, g_in, d_in, tick), refs = refs[: SIDE - 1], refs[SIDE - 1 : SIDE + 3], refs[SIDE + 3 :]
    backs, (row_scr, decay_scr, code_scr) = refs[:SIDE], refs[SIDE:]
    x, y = place()
    row_scr[...] = jnp.zeros_like(row_scr)
    decay_scr[...] = jnp.zeros_like(decay_scr)
    for shift, row in enumerate(rows, 1):
        source = lax.rem(y - shift + SIDE, SIDE)
        for k in range(QUARTER):
            aux = row[k, 64:80, :].astype(f32)
            row_scr[source, k] = decode(row[k, 0:64, :], aux[0:1])
            decay_scr[source, k] = jnp.broadcast_to(jnp.exp(aux[2:3] + aux[3:4] + aux[4:5]), (8, 128))
    for k in range(QUARTER):
        e_run = jnp.zeros((HEAD_DIM, 128), f32)
        f_run = jnp.zeros((HEAD_DIM, 128), f32)
        for n in range(SIDE):
            e_run = jnp.where(n < y, decay_scr[n, k][0:1] * e_run + row_scr[n, k], e_run)
            m = SIDE - 1 - n
            f_run = jnp.where(m > y, decay_scr[m, k][0:1] * f_run + row_scr[m, k], f_run)
        scales = [[None, None] for _ in range(SIDE)]
        for n in range(SIDE):
            m = SIDE - 1 - n
            code_scr[n, k, 0:64, :], scales[n][0] = encode(e_run)
            code_scr[m, k, 64:128, :], scales[m][1] = encode(f_run)
            e_run = jnp.exp(d_in[n, k][0:1]) * e_run + s_in[n, k]
            f_run = jnp.exp(d_in[m, k][0:1]) * f_run + g_in[m, k]
        at = iota((16, 128), 0)
        for n in range(SIDE):
            code_scr[n, k, 128:144, :] = jnp.where(at == 0, scales[n][0], scales[n][1]).astype(bf16)
    for shift, back in enumerate(backs):
        back[...] = code_scr[lax.rem(x + shift, SIDE)]


def block_kernel(
    first_pair, xs, gs, bs, cs, before, taps, cums, steps, after_this, skip,
    ys, dxs, slopes, xws, ges, bcs, slopes_bc, dbcs, sums,
    rows_scr, ds_scr, off_scr, diag_scr, cols_scr, pick_scr, sc_scr, row_scr, acc_scr,
):
    cum, step = cums[...], steps[...]
    shifted = cum - jnp.log(step)
    for head in range(HEADS):
        row_scr[head] = jnp.broadcast_to(cum[head : head + 1], (8, TOKENS))
        row_scr[HEADS + head] = jnp.broadcast_to(shifted[head : head + 1], (8, TOKENS))
    inner, outer, from_start, to_end, _ = decay_terms(cum, step)
    stacked = []
    for n, v in enumerate((cum, shifted, inner, outer, step, from_start, to_end)):
        stacked += [p.astype(f32) for p in split3(v)[: 3 if n < 2 else 2]]
    cols_scr[...] = jnp.concatenate(stacked, axis=0).T
    r, l = iota((256, 256), 0), iota((256, 256), 1)
    same = r % 2 == l // 128
    pick_scr[:, 0:256] = onehot((r < 48) & same)
    pick_scr[:, 256:512] = onehot((r >= 48) & (r < 96) & same)
    r, l = iota((256, 128), 0), iota((256, 128), 1)
    same = r % 2 == l // HEAD_DIM
    for n in range(5):
        pick_scr[:, 512 + 128 * n : 640 + 128 * n] = onehot(((r - 96) // 32 == n) & (r >= 96) & same)
    pair_of = (iota((TOKENS, 256), 1) % HEADS) // 2
    column = iota((256, 128), 1) - (iota((256, 128), 0) // HEAD_DIM) % 2
    rows_scr[8 - RIM : 8, :] = before[...].astype(f32)
    for n, (raw, lanes) in enumerate(((bs, B_LANES), (cs, C_LANES))):
        rows_scr[8:, lanes] = raw[...].astype(f32)
        act, slope = slope_of(conv_rows(rows_scr, taps[:, lanes], lanes))
        bcs[:, n * STATE : n * STATE + STATE] = act
        slopes_bc[:, n * STATE : n * STATE + STATE] = slope
    b, c = bcs[:, :STATE], bcs[:, STATE:]
    r, l = iota((SUB, SUB), 0), iota((SUB, SUB), 1)
    b2, c2 = split2(b), split2(c)

    def rows(parts, s):
        return tuple(p[s * SUB : s * SUB + SUB] for p in parts)

    for s in range(2):
        sc_scr[s] = jnp.where(r > l, dot3(rows(c2, s), rows(b2, s), NT), 0.0)
        sc_scr[2 + s] = jnp.where(l > r, dot3(rows(b2, s), rows(c2, s), NT), 0.0)
    off_scr[0] = jnp.concatenate(split2(dot3(rows(c2, 1), rows(b2, 0), NT)), axis=1)
    off_scr[1] = jnp.concatenate(split2(dot3(rows(b2, 0), rows(c2, 1), NT)), axis=1)
    ds_scr[...] = jnp.zeros_like(ds_scr)
    acc_scr[...] = jnp.zeros_like(acc_scr)
    diag = jnp.broadcast_to(jnp.sum(b * c, axis=1, keepdims=True), (TOKENS, 128))
    diag_scr[0] = diag
    diag_scr[1] = jnp.zeros((TOKENS, 128), f32)
    low = low_half((SUB, 128))
    zero = jnp.zeros((SUB, 128), bf16)

    def twice(hi, lo):
        return jnp.concatenate([jnp.concatenate([hi, lo], axis=1), jnp.concatenate([hi, zero], axis=1)], axis=0)

    def fold(v):
        return v[:, :128] + v[:, 128:]

    def pair_step(pair):
        lanes = pl.ds(pair * 128, 128)
        local = pl.ds((pair - first_pair) * 128, 128)
        head = 2 * pair
        rows_scr[8:, lanes] = xs[:, lanes].astype(f32)
        x, slope = slope_of(conv_rows(rows_scr, taps[:, lanes], lanes))
        slopes[:, local] = slope
        g = gs[:, lanes]
        gf = g.astype(f32)
        xh, xl = split2(x)
        cols = jnp.where(pair_of == pair, cols_scr[...], 0.0).astype(bf16)
        cum_cols = dot(cols, pick_scr[:, 0:256])
        shifted_cols = dot(cols, pick_scr[:, 256:512])
        inner_x, outer_x = (dot(cols, pick_scr[:, a : a + 128]) for a in (512, 640))
        step_x, start_x, end_x = (dot(cols, pick_scr[:, a : a + 128]) for a in (768, 896, 1024))
        for n, piece in enumerate(split2(x * end_x)):
            xws[n, :, local] = piece
        for n, piece in enumerate(split2(gf * start_x)):
            ges[n, :, local] = piece
        y_parts, dx_parts = [], []
        for s in range(2):
            at = slice(s * SUB, s * SUB + SUB)
            xh_s, xl_s, g_s = xh[at], xl[at], g[at]
            ms, ts, decays = [], [], []
            for k in range(2):
                row_cum = row_scr[head + k][0:1, at]
                row_shift = row_scr[HEADS + head + k][0:1, at]
                col_cum = cum_cols[at, k * 128 : k * 128 + 128]
                col_shift = shifted_cols[at, k * 128 : k * 128 + 128]
                decay = jnp.exp(jnp.where(r > l, col_cum - row_shift, NEG))
                decay_t = jnp.exp(jnp.where(l > r, row_cum - col_shift, NEG))
                decays.append(decay)
                ms.append(jnp.concatenate(split2(sc_scr[s] * decay), axis=1))
                ts.append(jnp.concatenate(split2(sc_scr[2 + s] * decay_t), axis=1))
            y2 = fold(dot(jnp.concatenate(ms, axis=0), twice(xh_s, xl_s)))
            dx2 = dot(jnp.concatenate(ts, axis=0), jnp.concatenate([g_s, g_s], axis=0))
            gf_s = g_s.astype(f32)
            g0 = jnp.where(low, gf_s, 0.0).astype(bf16)
            g1 = jnp.where(low, 0.0, gf_s).astype(bf16)
            g01 = jnp.concatenate([g0, g1], axis=0)
            dm = dot(jnp.concatenate([g01, g01], axis=1), jnp.concatenate([xh_s, xl_s], axis=1), NT)
            ds_scr[s] += dm[:SUB] * decays[0] + dm[SUB:] * decays[1]
            y_parts.append(jnp.where(low, y2[:SUB], y2[SUB:]))
            dx_parts.append(jnp.where(low, dx2[:SUB], dx2[SUB:]))
        xwh, xwl = split2(x[:SUB] * outer_x[:SUB])
        geh, gel = split2(gf[SUB:] * inner_x[SUB:])
        y_parts[1] += inner_x[SUB:] * fold(dot(off_scr[0], twice(xwh, xwl)))
        dx_parts[0] += outer_x[:SUB] * fold(dot(off_scr[1], twice(geh, gel)))
        ds_scr[2] += dot(jnp.concatenate([geh, gel], axis=1), jnp.concatenate([xwh, xwh], axis=1), NT) + dot(geh, xwl, NT)
        y = jnp.concatenate(y_parts, axis=0)
        dx = jnp.concatenate(dx_parts, axis=0)
        xg = x * gf
        xdx = x * dx
        total = acc_scr[...]
        for n, v in enumerate((gf * y - xdx, xdx, xg)):
            hot = onehot(column == n * HEADS + head)
            total += dot(jnp.concatenate(split2(v), axis=1), hot)
        acc_scr[...] = total
        diag_scr[1] += step_x * xg
        direct = jnp.where(low_half((TOKENS, 128)), skip[0, head], skip[0, head + 1]) + diag_scr[0] * step_x
        ys[:, local] = y + direct * x
        dxs[:, local] = dx + direct * gf

    for pair in range(first_pair, first_pair + PAIRS // 2):
        pair_step(pair)
    d_diag = jnp.sum(diag_scr[1], axis=1, keepdims=True)
    db = d_diag * c
    dc = d_diag * b
    for s in range(2):
        ds = jnp.where(r > l, ds_scr[s], 0.0)
        d2 = split2(ds)
        t2 = split2(ds.T)
        at = slice(s * SUB, s * SUB + SUB)
        dc_s = dc[at] + dot3(d2, rows(b2, s))
        db_s = db[at] + dot3(t2, rows(c2, s))
        if s == 0:
            db_s += dot3(split2(ds_scr[2].T), rows(c2, 1))
        else:
            dc_s += dot3(split2(ds_scr[2]), rows(b2, 0))
        dbcs[at, :STATE] = db_s
        dbcs[at, STATE:] = dc_s
    turned = acc_scr[...].T
    sums[0] = turned[0:HEADS]
    sums[1] = turned[HEADS : 2 * HEADS] / step + diag_scr[0].T[0:1] * turned[2 * HEADS : 3 * HEADS]


def wide_product(a2, cat, lanes):
    return dot(jnp.concatenate([a2[0], a2[0]], axis=1), cat[:, lanes]) + dot(a2[1], cat[:STATE, lanes])


def both_halves(n):
    per = PARTS // 2
    return n // per, pl.ds((n % per) * PART, PART)


def rim_kernel(*refs):
    backs, refs = refs[:SIDE], refs[SIDE:]
    bc, dx0, dx1, slope0, slope1, slope_bc, dbc0, dbc1, xw0, xw1, ge0, ge1, end16, e_cat, f_cat, rim = refs
    x, _ = place()
    for shift, back in enumerate(backs):
        q = lax.rem(x - shift + SIDE, SIDE)
        blocks = [[], []]
        for half in range(PART // 128):
            codes = []
            for k in range(2):
                slot = 2 * half + k
                aux = back[slot, 128:144, :].astype(f32)
                codes.append((decode(back[slot, 0:64, :], aux[0:1]), decode(back[slot, 64:128, :], aux[1:2])))
            for n in range(2):
                blocks[n].append(jnp.concatenate(join_heads(codes[0][n], codes[1][n]), axis=0))
        for n, cat in enumerate((e_cat, f_cat)):
            hi, lo = split2(jnp.concatenate(blocks[n], axis=1))
            cat[:STATE, quarter(q)] = hi
            cat[STATE:, quarter(q)] = lo
    b2 = split2(bc[0:16, :STATE])
    for n in range(PARTS):
        side, lanes = both_halves(n)
        dx, slope = ((dx0, slope0), (dx1, slope1))[side]
        d = (dx[0:16, lanes] + end16[:, part(n)] * wide_product(b2, f_cat, part(n))) * slope[0:16, lanes]
        rim[:, n * PART : n * PART + PART] = d[:RIM]
    for n, (v, cat) in enumerate((((xw0, xw1), f_cat), ((ge0, ge1), e_cat))):
        hi, lo = (jnp.concatenate([v[0][m, 0:16, :], v[1][m, 0:16, :]], axis=1) for m in range(2))
        both = dot(hi, cat[...], NT)
        d = both[:, :STATE] + both[:, STATE:] + dot(lo, cat[:STATE], NT)
        cut = slice(n * STATE, n * STATE + STATE)
        d = (dbc0[0:16, cut] + dbc1[0:16, cut] + d) * slope_bc[0:16, cut]
        rim[:, WIDTH + n * STATE : WIDTH + n * STATE + STATE] = d[:RIM]


def main_kernel(
    e_cat, f_cat, columns, bc, y0, y1, dx0, dx1, slope0, slope1, ge0, ge1, xw0, xw1, dbc0, dbc1, slope_bc,
    sums0, sums1, cums, steps, dts, bias, rate,
    y_out, dpre, dpre_bc, dt_out,
    ys, gdt, out_sems,
):
    b2, c2 = split2(bc[:, :STATE]), split2(bc[:, STATE:])
    grads = [[jnp.zeros((TOKENS, PART), f32), jnp.zeros((TOKENS, STATE), f32)] for _ in range(2)]
    total = jnp.zeros((TOKENS, 128), f32)
    both = jnp.zeros((8, 128), f32)
    out = []
    for n in range(PARTS):
        lanes = part(n)
        heads = n * PART // HEAD_DIM
        side, own = both_halves(n)
        y_in, dx, slope, ge, xw = ((y0, dx0, slope0, ge0, xw0), (y1, dx1, slope1, ge1, xw1))[side]
        start_x = dot(columns[...], spread_matrix(2, 128, 0, heads, HEAD_DIM, PART))
        end_x = dot(columns[...], spread_matrix(2, 128, 1, heads, HEAD_DIM, PART))
        ce = wide_product(c2, e_cat, lanes)
        bf = wide_product(b2, f_cat, lanes)
        ys[:, lanes] = y_in[:, own] + start_x * ce
        copy = pltpu.make_async_copy(ys.at[:, lanes], y_out.at[:, lanes], out_sems.at[n])
        copy.start()
        out.append(copy)
        dpre[:, lanes] = (dx[:, own] + end_x * bf) * slope[:, own]
        for grad, v, cat in zip(grads, (xw, ge), (f_cat, e_cat)):
            grad[0] += dot(v[0, :, own], cat[:, lanes], NT)
            grad[1] += dot(v[1, :, own], cat[:STATE, lanes], NT)
        for v, product, offset in ((xw, bf, 0), (ge, ce, HEADS)):
            hi, lo = split2((v[0, :, own].astype(f32) + v[1, :, own].astype(f32)) * product)
            hot = sum_matrix(PART, offset + heads)
            total += dot(hi, hot) + dot(lo, hot)
        e = e_cat[:STATE, lanes].astype(f32) + e_cat[STATE:, lanes].astype(f32)
        f = f_cat[:STATE, lanes].astype(f32) + f_cat[STATE:, lanes].astype(f32)
        hi, lo = split2(jnp.broadcast_to(jnp.sum(e * f, axis=0, keepdims=True), (8, PART)))
        hot = sum_matrix(PART, heads)
        both += dot(hi, hot) + dot(lo, hot)
    for n, grad in enumerate(grads):
        cut = slice(n * STATE, n * STATE + STATE)
        d = dbc0[:, cut] + dbc1[:, cut] + grad[0][:, :STATE] + grad[0][:, STATE:] + grad[1]
        dpre_bc[:, cut] = d * slope_bc[:, cut]
    turned = total.T
    later, kept = turned[0:HEADS], turned[HEADS : 2 * HEADS]
    r, c = iota((TOKENS, TOKENS), 0), iota((TOKENS, TOKENS), 1)
    suffix = onehot(r >= c)
    prefix = onehot(r < c)

    def summed(v, tri):
        hi, mid, lo = split3(v)
        return dot(lo, tri) + dot(mid, tri) + dot(hi, tri)

    cum, step = cums[...], steps[...]
    ends = jnp.exp(cum[:, SUB - 1 : SUB] + cum[:, TOKENS - 1 : TOKENS])
    local = sums0[0] + sums1[0]
    direct = sums0[1] + sums1[1]
    d_decay = summed(local + kept, suffix) + summed(later, prefix) + ends * to_column(both[0:1, 0:HEADS])
    d_step = direct + later / step - jnp.exp(to_column(rate[...])) * d_decay
    pre = dts[...].astype(f32) + to_column(bias[...])
    gdt[...] = d_step / (1.0 + jnp.exp(-pre))
    out.append(pltpu.make_async_copy(gdt, dt_out, out_sems.at[PARTS]))
    out[-1].start()
    wait(out)


def settle_kernel(dpre, dpre_bc, after, taps, gx_out, gb_out, gc_out, rows_scr, gx, gb, gc, out_sems):
    out = []

    def send(src, dst):
        copy = pltpu.make_async_copy(src, dst, out_sems.at[len(out)])
        copy.start()
        out.append(copy)

    rows_scr[TOKENS : TOKENS + RIM, :] = after[...]

    def unconv(d, lanes):
        rows_scr[0:TOKENS, lanes] = d
        v = taps[RIM : RIM + 1, lanes] * d
        for k in range(RIM):
            v += taps[k : k + 1, lanes] * rows_scr[RIM - k : RIM - k + TOKENS, lanes]
        return v

    for n in range(PARTS):
        lanes = part(n)
        gx[:, lanes] = unconv(dpre[:, lanes], lanes)
        send(gx.at[:, lanes], gx_out.at[:, lanes])
    gb[...] = unconv(dpre_bc[:, :STATE], B_LANES)
    send(gb, gb_out)
    gc[...] = unconv(dpre_bc[:, STATE:], C_LANES)
    send(gc, gc_out)
    wait(out)


VMEM = pl.BlockSpec(memory_space=pltpu.VMEM)
SMEM = pl.BlockSpec(memory_space=pltpu.SMEM)
HBM = pl.BlockSpec(memory_space=pltpu.HBM)


def call(kernel, ins, outs, scratch=(), sems=(), flops=0, mib=20):
    shapes = [jax.ShapeDtypeStruct(s, d) for s, d, _ in outs]
    moved = sum(a.size * a.dtype.itemsize for a, _ in ins) + sum(s.size * s.dtype.itemsize for s in shapes)
    return pl.pallas_call(
        kernel,
        out_shape=shapes,
        in_specs=[w for _, w in ins],
        out_specs=[w for _, _, w in outs],
        scratch_shapes=[pltpu.VMEM(s, d) for s, d in scratch] + [pltpu.SemaphoreType.DMA((n,)) for n in sems],
        compiler_params=pltpu.CompilerParams(vmem_limit_bytes=mib * 1024 * 1024),
        cost_estimate=pl.CostEstimate(flops=flops, bytes_accessed=moved, transcendentals=0),
    )(*[a for a, _ in ins])


def along_row(block, shift):
    return lax.ppermute(
        block, "context", [(SIDE * y + x, SIDE * y + (x + shift) % SIDE) for y in range(SIDE) for x in range(SIDE)]
    )


def along_column(block, shift):
    return lax.ppermute(
        block, "context", [(SIDE * y + x, SIDE * ((y + shift) % SIDE) + x) for y in range(SIDE) for x in range(SIDE)]
    )


def on_device(
    x_raw, b_raw, c_raw, dt_raw, dt_bias, a_log, skip_gain, conv_x, conv_b, conv_c, grad_y
):
    wide, slim, bc, narrow = (TOKENS, WIDTH), (HEADS, TOKENS), (TOKENS, 2 * STATE), (TOKENS, STATE)
    rim16, row = (16, WIDTH), (1, HEADS)
    dt_bias, a_log, skip_gain = (v.reshape(row) for v in (dt_bias, a_log, skip_gain))

    def near(*arrays):
        return [(a, VMEM) for a in arrays]

    (edge,) = call(
        edge_kernel, [(a, HBM) for a in (x_raw, b_raw, c_raw)], [((RIM, ALL), bf16, VMEM)], [((16, ALL), bf16)], [3],
        mib=60,
    )
    before = lax.ppermute(edge, "context", [(i, i + 1) for i in range(RANKS - 1)])
    sg, pre16, end16, ge16, taps, total, cum, step, columns = call(
        first_kernel,
        near(x_raw, grad_y, b_raw, c_raw, dt_raw, dt_bias, a_log, conv_x, conv_b, conv_c),
        [((2, STATE, WIDTH), f32, VMEM), ((16, ALL), f32, VMEM), (rim16, f32, VMEM), (rim16, f32, VMEM),
         ((4, ALL), f32, VMEM), ((HEADS, 8, 128), f32, VMEM), (slim, f32, VMEM), (slim, f32, VMEM),
         ((TOKENS, 128), bf16, VMEM)],
        [((TOKENS + 8, ALL), f32)],
        flops=2_000_000_000,
    )
    message = ((QUARTER, CHUNK, 128), bf16, VMEM)
    pays = call(
        send_kernel, near(before, sg, pre16, end16, ge16, taps, total), [message] * SIDE, [(rim16, f32), (rim16, f32)]
    )

    def block(first_pair, after_this):
        half = (TOKENS, WIDTH // 2)
        return call(
            functools.partial(block_kernel, first_pair),
            near(x_raw, grad_y, b_raw, c_raw, before, taps, cum, step, after_this) + [(skip_gain, SMEM)],
            [(half, f32, VMEM)] * 3 + [((2,) + half, bf16, VMEM)] * 2 + [(bc, f32, VMEM)] * 3
            + [((2,) + slim, f32, VMEM)],
            [((TOKENS + 8, ALL), f32), ((3, SUB, SUB), f32), ((2, SUB, 2 * SUB), bf16), ((2, TOKENS, 128), f32),
             ((TOKENS, 256), f32), ((256, 1152), bf16), ((4, SUB, SUB), f32), ((2 * HEADS, 8, TOKENS), f32),
             ((TOKENS, 128), f32)],
            flops=4_000_000_000,
        )

    got = [pays[0]] + [along_row(pays[shift], shift) for shift in (1, 2, 3)]
    y0, dx0, slope0, xw0, ge0, bcs, slope_bc, dbc0, sums0 = block(0, pays[0])
    *sends, s_all, g_all, d_all = call(
        row_kernel,
        near(*got, sums0),
        [((QUARTER, ROWMSG, 128), bf16, VMEM)] * (SIDE - 1)
        + [((SIDE, QUARTER, HEAD_DIM, 128), f32, VMEM)] * 2 + [((SIDE, QUARTER, 8, 128), f32, VMEM)],
    )
    rows = [along_column(sends[shift - 1], shift) for shift in (1, 2, 3)]
    y1, dx1, slope1, xw1, ge1, _, _, dbc1, sums1 = block(PAIRS // 2, d_all)
    answers = call(
        column_kernel,
        near(*rows, s_all, g_all, d_all, sums1),
        [message] * SIDE,
        [((SIDE, QUARTER, HEAD_DIM, 128), f32), ((SIDE, QUARTER, 8, 128), f32), ((SIDE, QUARTER, CHUNK, 128), bf16)],
    )
    backs = [answers[0]] + [along_row(answers[shift], shift) for shift in (1, 2, 3)]
    cat = ((2 * STATE, WIDTH), bf16)
    e_cat, f_cat, rim = call(
        rim_kernel,
        near(*backs, bcs, dx0, dx1, slope0, slope1, slope_bc, dbc0, dbc1, xw0, xw1, ge0, ge1, end16),
        [(*cat, VMEM), (*cat, VMEM), ((RIM, ALL), f32, VMEM)],
    )
    after = lax.ppermute(rim, "context", [(i, i - 1) for i in range(1, RANKS)])
    y_out, dpre, dpre_bc, grad_dt = call(
        main_kernel,
        near(e_cat, f_cat, columns, bcs, y0, y1, dx0, dx1, slope0, slope1, ge0, ge1, xw0, xw1, dbc0, dbc1, slope_bc,
             sums0, sums1, cum, step, dt_raw, dt_bias, a_log),
        [(wide, f32, HBM), (wide, f32, VMEM), (bc, f32, VMEM), (slim, f32, HBM)],
        [(wide, f32), (slim, f32)],
        [PARTS + 1],
        flops=2_000_000_000,
    )
    grad_x, grad_b, grad_c = call(
        settle_kernel,
        near(dpre, dpre_bc, after, taps),
        [(wide, f32, HBM), (narrow, f32, HBM), (narrow, f32, HBM)],
        [((TOKENS + 8, ALL), f32), (wide, f32), (narrow, f32), (narrow, f32)],
        [PARTS + 2],
    )
    return (y_out, grad_x, grad_b, grad_c, grad_dt)


def solution(mesh):
    tokens = P(("dp", "context"), "tensor")
    heads = P("tensor", ("dp", "context"))
    one, taps = P("tensor"), P(None, "tensor")
    return jax.shard_map(
        on_device,
        mesh=mesh,
        in_specs=(tokens, tokens, tokens, heads, one, one, one, taps, taps, taps, tokens),
        out_specs=(tokens, tokens, tokens, tokens, heads),
        check_vma=False,
    )
```

```python
import functools

import jax
import jax.numpy as jnp
from jax import lax
from jax.experimental import pallas as pl
from jax.experimental.pallas import tpu as pltpu
from jax.sharding import PartitionSpec as P

f32 = jnp.float32
bf16 = jnp.bfloat16

TOKENS = 256
SUB = 128
HEADS = 16
HEAD_DIM = 64
STATE = 128
WIDTH = HEADS * HEAD_DIM
PAIRS = HEADS // 2
RIM = 3
RANKS = 16
SIDE = 4
QUARTER = HEADS // SIDE
ROWMSG = 80
CHUNK = 144
ALL = WIDTH + 2 * STATE
PART = 256
PARTS = WIDTH // PART
NEG = -1e30
CODE_SPAN = 248.0

NN = ((1,), (0,))
NT = ((1,), (1,))
TN = ((0,), (0,))


def dot(a, b, dims=NN):
    return lax.dot_general(a, b, (dims, ((), ())), preferred_element_type=f32)


def split2(v):
    hi = v.astype(bf16)
    return hi, (v - hi.astype(f32)).astype(bf16)


def split3(v):
    hi = v.astype(bf16)
    rest = v - hi.astype(f32)
    mid = rest.astype(bf16)
    return hi, mid, (rest - mid.astype(f32)).astype(bf16)


def dot3(a, b, dims=NN):
    return dot(a[0], b[0], dims) + dot(a[1], b[0], dims) + dot(a[0], b[1], dims)


def iota(shape, axis):
    return lax.broadcasted_iota(jnp.int32, shape, axis)


def onehot(mask):
    return jnp.where(mask, 1.0, 0.0).astype(bf16)


def to_column(row):
    n = row.shape[1]
    eye = iota((n, n), 0) == iota((n, n), 1)
    return jnp.sum(jnp.where(eye, row, 0.0), axis=1, keepdims=True)


def low_half(shape):
    return iota(shape, 1) < HEAD_DIM


def swap_halves(v):
    return pltpu.roll(v, HEAD_DIM, 1)


def encode(v):
    top = jnp.max(jnp.abs(v), axis=0, keepdims=True)
    scale = (jnp.maximum(top, 1e-30) * 1.01).astype(bf16).astype(f32)
    unit = jnp.abs(v) * (CODE_SPAN / scale)
    size = jnp.exp2(unit - CODE_SPAN / 2)
    return jnp.where(v < 0, -size, size).astype(bf16), scale


def decode(code, scale):
    v = code.astype(f32)
    unit = jnp.log2(jnp.abs(v)) + CODE_SPAN / 2
    size = unit * (scale * (1.0 / CODE_SPAN))
    return jnp.where(v < 0, -size, size)


def split_heads(pair):
    top, bottom = pair[:HEAD_DIM], pair[HEAD_DIM:]
    low = low_half(top.shape)
    return (
        jnp.where(low, top, swap_halves(bottom)),
        jnp.where(low, swap_halves(top), bottom),
    )


def join_heads(first, second):
    low = low_half(first.shape)
    return (
        jnp.where(low, first, swap_halves(second)),
        jnp.where(low, swap_halves(first), second),
    )


def stack_columns(arrays):
    stacked = jnp.concatenate(list(arrays), axis=0)
    parts = [p.astype(f32) for p in split3(stacked)]
    rows = 3 * stacked.shape[0]
    full = 128 if rows <= 128 else 256
    parts.append(jnp.zeros((full - rows, TOKENS), f32))
    return jnp.concatenate(parts, axis=0).T.astype(bf16)


def spread_matrix(count, full, which, first_head, lanes_per_head, lanes):
    r, l = iota((full, lanes), 0), iota((full, lanes), 1)
    rows = r - (r // (count * HEADS)) * (count * HEADS)
    return onehot((r < 3 * count * HEADS) & (rows - l // lanes_per_head == which * HEADS + first_head))


def sum_matrix(rows, offset):
    r, l = iota((rows, 128), 0), iota((rows, 128), 1)
    return onehot(r // HEAD_DIM + offset == l)


def decay_terms(cum, step):
    first = iota(cum.shape, 1) < SUB
    end0 = cum[:, SUB - 1 : SUB]
    end1 = cum[:, TOKENS - 1 : TOKENS]
    inner = jnp.exp(cum)
    outer = jnp.exp(jnp.where(first, end0, end1) - cum) * step
    from_start = jnp.where(first, inner, inner * jnp.exp(end0))
    to_end = jnp.where(first, outer * jnp.exp(end1), outer)
    return inner, outer, from_start, to_end, end0 + end1


def begin(moves, sems):
    copies = [pltpu.make_async_copy(a, b, sems.at[n]) for n, (a, b) in enumerate(moves)]
    for copy in copies:
        copy.start()
    return copies


def wait(copies):
    for copy in copies:
        copy.wait()


def part(n):
    return pl.ds(n * PART, PART)


def silu_of(v):
    return v / (1.0 + jnp.exp(-v))


def slope_of(v):
    gate = 1.0 / (1.0 + jnp.exp(-v))
    return v * gate, gate * (1.0 + v * (1.0 - gate))


def conv_rows(rows_scr, taps, lanes):
    v = taps[0:1] * rows_scr[8 - RIM : 8 - RIM + TOKENS, lanes]
    for k in range(1, RIM + 1):
        v += taps[k : k + 1] * rows_scr[8 - RIM + k : 8 - RIM + k + TOKENS, lanes]
    return v


B_LANES = pl.ds(WIDTH, STATE)
C_LANES = pl.ds(WIDTH + STATE, STATE)


def edge_kernel(x_raw, b_raw, c_raw, edge, scr, sems):
    rows = pl.ds(TOKENS - 16, 16)
    wait(
        begin(
            [
                (x_raw.at[rows, :], scr.at[:, pl.ds(0, WIDTH)]),
                (b_raw.at[rows, :], scr.at[:, B_LANES]),
                (c_raw.at[rows, :], scr.at[:, C_LANES]),
            ],
            sems,
        )
    )
    edge[...] = scr[...].astype(f32)[16 - RIM :].astype(bf16)


def first_kernel(
    xs, gs, bs, cs, dts, bias, rate, taps_x, taps_b, taps_c,
    sg, pre16, end16, ge16, taps_out, total_out, cum_out, step_out, columns_out,
    rows_scr,
):
    pre = dts[...].astype(f32) + to_column(bias[...])
    step = jnp.maximum(pre, 0.0) + jnp.log1p(jnp.exp(-jnp.abs(pre)))
    log_decay = -jnp.exp(to_column(rate[...])) * step
    r, c = iota((TOKENS, TOKENS), 0), iota((TOKENS, TOKENS), 1)
    upto = onehot((r <= c) & (r // SUB == c // SUB))
    parts = split3(log_decay)
    cum = dot(parts[2], upto) + dot(parts[1], upto) + dot(parts[0], upto)
    cum_out[...] = cum
    step_out[...] = step
    _, _, from_start, to_end, total = decay_terms(cum, step)
    for head in range(HEADS):
        total_out[head] = jnp.broadcast_to(total[head : head + 1], (8, 128))
    columns = stack_columns([from_start, to_end])
    columns_out[...] = columns
    taps_out[:, 0:WIDTH] = taps_x[...]
    taps_out[:, WIDTH : WIDTH + STATE] = taps_b[...]
    taps_out[:, WIDTH + STATE :] = taps_c[...]
    rows_scr[0:8, :] = jnp.zeros((8, ALL), f32)
    known = iota((TOKENS, 128), 0) >= 16
    turned = []
    for raw, taps, lanes in ((bs, taps_b, B_LANES), (cs, taps_c, C_LANES)):
        rows_scr[8:, lanes] = raw[...].astype(f32)
        v = conv_rows(rows_scr, taps[...], lanes)
        pre16[:, lanes] = v[:16]
        turned.append(split2(jnp.where(known, silu_of(v), 0.0).T))
    bt, ct = turned
    for n in range(PARTS):
        lanes = part(n)
        heads = n * PART // HEAD_DIM
        start_x = dot(columns, spread_matrix(2, 128, 0, heads, HEAD_DIM, PART))
        end_x = dot(columns, spread_matrix(2, 128, 1, heads, HEAD_DIM, PART))
        rows_scr[8:, lanes] = xs[:, lanes].astype(f32)
        v = conv_rows(rows_scr, taps_x[:, lanes], lanes)
        pre16[:, lanes] = v[:16]
        end16[:, lanes] = end_x[:16]
        xw = silu_of(v) * end_x
        ge = gs[:, lanes].astype(f32) * start_x
        ge16[:, lanes] = ge[:16]
        sg[0, :, lanes] = dot3(bt, split2(xw))
        sg[1, :, lanes] = dot3(ct, split2(ge))


def quarter(q):
    return pl.ds(pl.multiple_of(q * PART, PART), PART)


def place():
    here = lax.axis_index("context")
    return lax.rem(here, SIDE), lax.div(here, SIDE)


def write_aux(scales, total):
    at = iota((16, 128), 0)
    aux = jnp.where(at == 0, scales[0], scales[-1])
    for m, piece in enumerate(split3(total)):
        aux = jnp.where(at == 2 + m, piece.astype(f32), aux)
    return aux.astype(bf16)


def send_kernel(before, sg, pre16, end16, ge16, taps, total, *refs):
    pays, (xw_scr, ge_scr) = refs[:SIDE], refs[SIDE:]
    halo = before[...].astype(f32)
    v = pre16[...]
    at = iota((16, ALL), 0)
    for row in range(RIM):
        more = taps[0:1] * halo[row : row + 1]
        for k in range(1, RIM - row):
            more += taps[k : k + 1] * halo[row + k : row + k + 1]
        v += jnp.where(at == row, more, 0.0)
    act = silu_of(v)
    xw_scr[...] = act[:, :WIDTH] * end16[...]
    ge_scr[...] = ge16[...]
    b = split2(act[:, WIDTH : WIDTH + STATE])
    c = split2(act[:, WIDTH + STATE :])
    x, _ = place()
    for shift, pay in enumerate(pays):
        q = lax.rem(x + shift, SIDE)
        lanes = quarter(q)
        s = sg[0, :, lanes] + dot3(b, split2(xw_scr[:, lanes]), TN)
        g = sg[1, :, lanes] + dot3(c, split2(ge_scr[:, lanes]), TN)
        for half in range(PART // 128):
            s_heads = split_heads(s[:, half * 128 : half * 128 + 128])
            g_heads = split_heads(g[:, half * 128 : half * 128 + 128])
            for k in range(2):
                slot = 2 * half + k
                s_code, s_scale = encode(s_heads[k])
                g_code, g_scale = encode(g_heads[k])
                pay[slot, 0:64, :] = s_code
                pay[slot, 64:128, :] = g_code
                pay[slot, 128:144, :] = write_aux((s_scale, g_scale), total[q * QUARTER + slot][0:1])


def row_kernel(*refs):
    pays, tick, refs = refs[:SIDE], refs[SIDE], refs[SIDE + 1 :]
    (*sends, s_out, g_out, d_out) = refs
    x, y = place()
    for shift, pay in enumerate(pays):
        source = lax.rem(x - shift + SIDE, SIDE)
        for k in range(QUARTER):
            aux = pay[k, 128:144, :].astype(f32)
            s_out[source, k] = decode(pay[k, 0:64, :], aux[0:1])
            g_out[source, k] = decode(pay[k, 64:128, :], aux[1:2])
            d_out[source, k] = jnp.broadcast_to(aux[2:3] + aux[3:4] + aux[4:5], (8, 128))
    for k in range(QUARTER):
        s_run, g_run = s_out[0, k], g_out[SIDE - 1, k]
        for n in range(1, SIDE):
            s_run = jnp.exp(d_out[n, k][0:1]) * s_run + s_out[n, k]
            m = SIDE - 1 - n
            g_run = jnp.exp(d_out[m, k][0:1]) * g_run + g_out[m, k]
        total = sum(d_out[n, k][0:1] for n in range(SIDE))
        for shift, message in enumerate(sends, 1):
            code, scale = encode(jnp.where(y + shift < SIDE, s_run, g_run))
            message[k, 0:64, :] = code
            message[k, 64:80, :] = write_aux((scale,), total)


def column_kernel(*refs):
    rows, (s_in, g_in, d_in, tick), refs = refs[: SIDE - 1], refs[SIDE - 1 : SIDE + 3], refs[SIDE + 3 :]
    backs, (row_scr, decay_scr, code_scr) = refs[:SIDE], refs[SIDE:]
    x, y = place()
    row_scr[...] = jnp.zeros_like(row_scr)
    decay_scr[...] = jnp.zeros_like(decay_scr)
    for shift, row in enumerate(rows, 1):
        source = lax.rem(y - shift + SIDE, SIDE)
        for k in range(QUARTER):
            aux = row[k, 64:80, :].astype(f32)
            row_scr[source, k] = decode(row[k, 0:64, :], aux[0:1])
            decay_scr[source, k] = jnp.broadcast_to(jnp.exp(aux[2:3] + aux[3:4] + aux[4:5]), (8, 128))
    for k in range(QUARTER):
        e_run = jnp.zeros((HEAD_DIM, 128), f32)
        f_run = jnp.zeros((HEAD_DIM, 128), f32)
        for n in range(SIDE):
            e_run = jnp.where(n < y, decay_scr[n, k][0:1] * e_run + row_scr[n, k], e_run)
            m = SIDE - 1 - n
            f_run = jnp.where(m > y, decay_scr[m, k][0:1] * f_run + row_scr[m, k], f_run)
        scales = [[None, None] for _ in range(SIDE)]
        for n in range(SIDE):
            m = SIDE - 1 - n
            code_scr[n, k, 0:64, :], scales[n][0] = encode(e_run)
            code_scr[m, k, 64:128, :], scales[m][1] = encode(f_run)
            e_run = jnp.exp(d_in[n, k][0:1]) * e_run + s_in[n, k]
            f_run = jnp.exp(d_in[m, k][0:1]) * f_run + g_in[m, k]
        at = iota((16, 128), 0)
        for n in range(SIDE):
            code_scr[n, k, 128:144, :] = jnp.where(at == 0, scales[n][0], scales[n][1]).astype(bf16)
    for shift, back in enumerate(backs):
        back[...] = code_scr[lax.rem(x + shift, SIDE)]


def block_setup(bs, cs, taps, cums, steps, rows_scr, shared):
    bcs, slopes_bc, sc_scr, off_scr, cols_scr, pick_scr, row_scr, diag_scr, ds, acc, dg = shared

    def rows(parts, s):
        return tuple(p[s * SUB : s * SUB + SUB] for p in parts)

    cum, step = cums[...], steps[...]
    shifted = cum - jnp.log(step)
    for head in range(HEADS):
        row_scr[head] = jnp.broadcast_to(cum[head : head + 1], (8, TOKENS))
        row_scr[HEADS + head] = jnp.broadcast_to(shifted[head : head + 1], (8, TOKENS))
    inner, outer, from_start, to_end, _ = decay_terms(cum, step)
    stacked = []
    for n, v in enumerate((cum, shifted, inner, outer, step, from_start, to_end)):
        stacked += [p.astype(f32) for p in split3(v)[: 3 if n < 2 else 2]]
    cols_scr[...] = jnp.concatenate(stacked, axis=0).T
    r, l = iota((256, 256), 0), iota((256, 256), 1)
    same = r % 2 == l // 128
    pick_scr[:, 0:256] = onehot((r < 48) & same)
    pick_scr[:, 256:512] = onehot((r >= 48) & (r < 96) & same)
    r, l = iota((256, 128), 0), iota((256, 128), 1)
    same = r % 2 == l // HEAD_DIM
    for n in range(5):
        pick_scr[:, 512 + 128 * n : 640 + 128 * n] = onehot(((r - 96) // 32 == n) & (r >= 96) & same)
    for n, (raw, lanes) in enumerate(((bs, B_LANES), (cs, C_LANES))):
        rows_scr[8:, lanes] = raw[...].astype(f32)
        act, slope = slope_of(conv_rows(rows_scr, taps[:, lanes], lanes))
        bcs[:, n * STATE : n * STATE + STATE] = act
        slopes_bc[:, n * STATE : n * STATE + STATE] = slope
    b, c = bcs[:, :STATE], bcs[:, STATE:]
    r, l = iota((SUB, SUB), 0), iota((SUB, SUB), 1)
    b2, c2 = split2(b), split2(c)

    for s in range(2):
        sc_scr[s] = jnp.where(r > l, dot3(rows(c2, s), rows(b2, s), NT), 0.0)
        sc_scr[2 + s] = jnp.where(l > r, dot3(rows(b2, s), rows(c2, s), NT), 0.0)
    off_scr[0] = jnp.concatenate(split2(dot3(rows(c2, 1), rows(b2, 0), NT)), axis=1)
    off_scr[1] = jnp.concatenate(split2(dot3(rows(b2, 0), rows(c2, 1), NT)), axis=1)
    ds[...] = jnp.zeros_like(ds)
    acc[...] = jnp.zeros_like(acc)
    diag = jnp.broadcast_to(jnp.sum(b * c, axis=1, keepdims=True), (TOKENS, 128))
    diag_scr[...] = diag
    dg[...] = jnp.zeros_like(dg)


def block_pairs(first_pair, count, xs, gs, taps, skip, outs, rows_scr, shared):
    ys, dxs, slopes, xws, ges = outs
    _, _, sc_scr, off_scr, cols_scr, pick_scr, row_scr, diag_scr, ds, acc, dg = shared
    r, l = iota((SUB, SUB), 0), iota((SUB, SUB), 1)
    low = low_half((SUB, 128))
    zero = jnp.zeros((SUB, 128), bf16)
    pair_of = (iota((TOKENS, 256), 1) % HEADS) // 2
    column = iota((256, 128), 1) - (iota((256, 128), 0) // HEAD_DIM) % 2

    def twice(hi, lo):
        return jnp.concatenate([jnp.concatenate([hi, lo], axis=1), jnp.concatenate([hi, zero], axis=1)], axis=0)

    def fold(v):
        return v[:, :128] + v[:, 128:]

    def pair_step(pair):
        lanes = pl.ds(pair * 128, 128)
        local = pl.ds((pair - first_pair) * 128, 128)
        head = 2 * pair
        rows_scr[8:, lanes] = xs[:, lanes].astype(f32)
        x, slope = slope_of(conv_rows(rows_scr, taps[:, lanes], lanes))
        slopes[:, local] = slope
        g = gs[:, lanes]
        gf = g.astype(f32)
        xh, xl = split2(x)
        cols = jnp.where(pair_of == pair, cols_scr[...], 0.0).astype(bf16)
        cum_cols = dot(cols, pick_scr[:, 0:256])
        shifted_cols = dot(cols, pick_scr[:, 256:512])
        inner_x, outer_x = (dot(cols, pick_scr[:, a : a + 128]) for a in (512, 640))
        step_x, start_x, end_x = (dot(cols, pick_scr[:, a : a + 128]) for a in (768, 896, 1024))
        for n, piece in enumerate(split2(x * end_x)):
            xws[n, :, local] = piece
        for n, piece in enumerate(split2(gf * start_x)):
            ges[n, :, local] = piece
        y_parts, dx_parts = [], []
        for s in range(2):
            at = slice(s * SUB, s * SUB + SUB)
            xh_s, xl_s, g_s = xh[at], xl[at], g[at]
            ms, ts, decays = [], [], []
            for k in range(2):
                row_cum = row_scr[head + k][0:1, at]
                row_shift = row_scr[HEADS + head + k][0:1, at]
                col_cum = cum_cols[at, k * 128 : k * 128 + 128]
                col_shift = shifted_cols[at, k * 128 : k * 128 + 128]
                decay = jnp.exp(jnp.where(r > l, col_cum - row_shift, NEG))
                decay_t = jnp.exp(jnp.where(l > r, row_cum - col_shift, NEG))
                decays.append(decay)
                ms.append(jnp.concatenate(split2(sc_scr[s] * decay), axis=1))
                ts.append(jnp.concatenate(split2(sc_scr[2 + s] * decay_t), axis=1))
            y2 = fold(dot(jnp.concatenate(ms, axis=0), twice(xh_s, xl_s)))
            dx2 = dot(jnp.concatenate(ts, axis=0), jnp.concatenate([g_s, g_s], axis=0))
            gf_s = g_s.astype(f32)
            g0 = jnp.where(low, gf_s, 0.0).astype(bf16)
            g1 = jnp.where(low, 0.0, gf_s).astype(bf16)
            g01 = jnp.concatenate([g0, g1], axis=0)
            dm = dot(jnp.concatenate([g01, g01], axis=1), jnp.concatenate([xh_s, xl_s], axis=1), NT)
            ds[s] += dm[:SUB] * decays[0] + dm[SUB:] * decays[1]
            y_parts.append(jnp.where(low, y2[:SUB], y2[SUB:]))
            dx_parts.append(jnp.where(low, dx2[:SUB], dx2[SUB:]))
        xwh, xwl = split2(x[:SUB] * outer_x[:SUB])
        geh, gel = split2(gf[SUB:] * inner_x[SUB:])
        y_parts[1] += inner_x[SUB:] * fold(dot(off_scr[0], twice(xwh, xwl)))
        dx_parts[0] += outer_x[:SUB] * fold(dot(off_scr[1], twice(geh, gel)))
        ds[2] += dot(jnp.concatenate([geh, gel], axis=1), jnp.concatenate([xwh, xwh], axis=1), NT) + dot(geh, xwl, NT)
        y = jnp.concatenate(y_parts, axis=0)
        dx = jnp.concatenate(dx_parts, axis=0)
        xg = x * gf
        xdx = x * dx
        total = acc[...]
        for n, v in enumerate((gf * y - xdx, xdx, xg)):
            hot = onehot(column == n * HEADS + head)
            total += dot(jnp.concatenate(split2(v), axis=1), hot)
        acc[...] = total
        dg[...] += step_x * xg
        direct = jnp.where(low_half((TOKENS, 128)), skip[:, head : head + 1], skip[:, head + 1 : head + 2]) + diag_scr[...] * step_x
        ys[:, local] = y + direct * x
        dxs[:, local] = dx + direct * gf

    for pair in range(first_pair, first_pair + count):
        pair_step(pair)


def block_finish(steps, dbcs, sums, shared):
    bcs, _, _, _, _, _, _, diag_scr, ds, acc, dg = shared
    step = steps[...]
    b, c = bcs[:, :STATE], bcs[:, STATE:]
    b2, c2 = split2(b), split2(c)
    r, l = iota((SUB, SUB), 0), iota((SUB, SUB), 1)

    def rows(parts, s):
        return tuple(p[s * SUB : s * SUB + SUB] for p in parts)

    d_diag = jnp.sum(dg[...], axis=1, keepdims=True)
    db = d_diag * c
    dc = d_diag * b
    for s in range(2):
        d = jnp.where(r > l, ds[s], 0.0)
        d2 = split2(d)
        t2 = split2(d.T)
        at = slice(s * SUB, s * SUB + SUB)
        dc_s = dc[at] + dot3(d2, rows(b2, s))
        db_s = db[at] + dot3(t2, rows(c2, s))
        if s == 0:
            db_s += dot3(split2(ds[2].T), rows(c2, 1))
        else:
            dc_s += dot3(split2(ds[2]), rows(b2, 0))
        dbcs[at, :STATE] = db_s
        dbcs[at, STATE:] = dc_s
    turned = acc[...].T
    sums[0] = turned[0:HEADS]
    sums[1] = turned[HEADS : 2 * HEADS] / step + diag_scr[...].T[0:1] * turned[2 * HEADS : 3 * HEADS]


def block_kernel(first_pair, count, *refs):
    (xs, gs, bs, cs, before, taps, cums, steps, skip, _), refs = refs[:10], refs[10:]
    rows_scr, refs = refs[-1], refs[:-1]
    rows_scr[8 - RIM : 8, :] = before[...].astype(f32)
    if first_pair == 0:
        outs, shared = refs[:5], refs[5:]
        block_setup(bs, cs, taps, cums, steps, rows_scr, shared)
    else:
        (*kept, ds_in, acc_in, dg_in), refs = refs[:11], refs[11:]
        outs, (ds, acc, dg) = refs[:5], refs[-3:]
        ds[...] = ds_in[...]
        acc[...] = acc_in[...]
        dg[...] = dg_in[...]
        shared = (*kept, ds, acc, dg)
    block_pairs(first_pair, count, xs, gs, taps, skip, outs, rows_scr, shared)
    if first_pair + count == PAIRS:
        block_finish(steps, refs[5], refs[6], shared)


def wide_product(a2, cat, lanes):
    return dot(jnp.concatenate([a2[0], a2[0]], axis=1), cat[:, lanes]) + dot(a2[1], cat[:STATE, lanes])


GROUP_PAIRS = (3, 2, 3)


def columns_of(refs, n, *lead):
    pieces = []
    for pair in range(2 * n, 2 * n + 2):
        group = 0
        while pair >= GROUP_PAIRS[group]:
            pair -= GROUP_PAIRS[group]
            group += 1
        pieces.append(refs[group][(*lead, slice(pair * 128, pair * 128 + 128))])
    return jnp.concatenate(pieces, axis=1)


def rim_kernel(*refs):
    backs, refs = refs[:SIDE], refs[SIDE:]
    (bc, slope_bc, dbc, end16), refs = refs[:4], refs[4:]
    dxs, slopes, xws, ges, (e_cat, f_cat, rim) = refs[:3], refs[3:6], refs[6:9], refs[9:12], refs[12:]
    x, _ = place()
    for shift, back in enumerate(backs):
        q = lax.rem(x - shift + SIDE, SIDE)
        blocks = [[], []]
        for half in range(PART // 128):
            codes = []
            for k in range(2):
                slot = 2 * half + k
                aux = back[slot, 128:144, :].astype(f32)
                codes.append((decode(back[slot, 0:64, :], aux[0:1]), decode(back[slot, 64:128, :], aux[1:2])))
            for n in range(2):
                blocks[n].append(jnp.concatenate(join_heads(codes[0][n], codes[1][n]), axis=0))
        for n, cat in enumerate((e_cat, f_cat)):
            hi, lo = split2(jnp.concatenate(blocks[n], axis=1))
            cat[:STATE, quarter(q)] = hi
            cat[STATE:, quarter(q)] = lo
    b2 = split2(bc[0:16, :STATE])
    for n in range(PARTS):
        top = slice(0, 16)
        d = columns_of(dxs, n, top) + end16[:, part(n)] * wide_product(b2, f_cat, part(n))
        d = d * columns_of(slopes, n, top)
        rim[:, n * PART : n * PART + PART] = d[:RIM]
    for n, (v, cat) in enumerate(((xws, f_cat), (ges, e_cat))):
        hi, lo = (jnp.concatenate([w[m, 0:16, :] for w in v], axis=1) for m in range(2))
        both = dot(hi, cat[...], NT)
        d = both[:, :STATE] + both[:, STATE:] + dot(lo, cat[:STATE], NT)
        cut = slice(n * STATE, n * STATE + STATE)
        d = (dbc[0:16, cut] + d) * slope_bc[0:16, cut]
        rim[:, WIDTH + n * STATE : WIDTH + n * STATE + STATE] = d[:RIM]


def main_kernel(*refs):
    (e_cat, f_cat, columns, bc, dbc, slope_bc, sums, cums, steps, dts, bias, rate), refs = refs[:12], refs[12:]
    groups, (y_out, dpre, dpre_bc, dt_out, ys, gdt, out_sems) = refs[:15], refs[15:]
    b2, c2 = split2(bc[:, :STATE]), split2(bc[:, STATE:])
    grads = [[jnp.zeros((TOKENS, PART), f32), jnp.zeros((TOKENS, STATE), f32)] for _ in range(2)]
    total = jnp.zeros((TOKENS, 128), f32)
    both = jnp.zeros((8, 128), f32)
    whole = slice(None)
    out = []
    for n in range(PARTS):
        lanes = part(n)
        heads = n * PART // HEAD_DIM
        y_in, dx, slope = (columns_of(groups[k::5], n, whole) for k in range(3))
        xw, ge = ([columns_of(groups[k::5], n, m, whole) for m in range(2)] for k in (3, 4))
        start_x = dot(columns[...], spread_matrix(2, 128, 0, heads, HEAD_DIM, PART))
        end_x = dot(columns[...], spread_matrix(2, 128, 1, heads, HEAD_DIM, PART))
        ce = wide_product(c2, e_cat, lanes)
        bf = wide_product(b2, f_cat, lanes)
        ys[:, lanes] = y_in + start_x * ce
        copy = pltpu.make_async_copy(ys.at[:, lanes], y_out.at[:, lanes], out_sems.at[n])
        copy.start()
        out.append(copy)
        dpre[:, lanes] = (dx + end_x * bf) * slope
        for grad, v, cat in zip(grads, (xw, ge), (f_cat, e_cat)):
            grad[0] += dot(v[0], cat[:, lanes], NT)
            grad[1] += dot(v[1], cat[:STATE, lanes], NT)
        for v, product, offset in ((xw, bf, 0), (ge, ce, HEADS)):
            hi, lo = split2((v[0].astype(f32) + v[1].astype(f32)) * product)
            hot = sum_matrix(PART, offset + heads)
            total += dot(hi, hot) + dot(lo, hot)
        e = e_cat[:STATE, lanes].astype(f32) + e_cat[STATE:, lanes].astype(f32)
        f = f_cat[:STATE, lanes].astype(f32) + f_cat[STATE:, lanes].astype(f32)
        hi, lo = split2(jnp.broadcast_to(jnp.sum(e * f, axis=0, keepdims=True), (8, PART)))
        hot = sum_matrix(PART, heads)
        both += dot(hi, hot) + dot(lo, hot)
    for n, grad in enumerate(grads):
        cut = slice(n * STATE, n * STATE + STATE)
        d = dbc[:, cut] + grad[0][:, :STATE] + grad[0][:, STATE:] + grad[1]
        dpre_bc[:, cut] = d * slope_bc[:, cut]
    turned = total.T
    later, kept = turned[0:HEADS], turned[HEADS : 2 * HEADS]
    r, c = iota((TOKENS, TOKENS), 0), iota((TOKENS, TOKENS), 1)
    suffix = onehot(r >= c)
    prefix = onehot(r < c)

    def summed(v, tri):
        hi, mid, lo = split3(v)
        return dot(lo, tri) + dot(mid, tri) + dot(hi, tri)

    cum, step = cums[...], steps[...]
    ends = jnp.exp(cum[:, SUB - 1 : SUB] + cum[:, TOKENS - 1 : TOKENS])
    d_decay = summed(sums[0] + kept, suffix) + summed(later, prefix) + ends * to_column(both[0:1, 0:HEADS])
    d_step = sums[1] + later / step - jnp.exp(to_column(rate[...])) * d_decay
    pre = dts[...].astype(f32) + to_column(bias[...])
    gdt[...] = d_step / (1.0 + jnp.exp(-pre))
    out.append(pltpu.make_async_copy(gdt, dt_out, out_sems.at[PARTS]))
    out[-1].start()
    wait(out)


def settle_kernel(dpre, dpre_bc, after, taps, gx_out, gb_out, gc_out, rows_scr, gx, gb, gc, out_sems):
    out = []

    def send(src, dst):
        copy = pltpu.make_async_copy(src, dst, out_sems.at[len(out)])
        copy.start()
        out.append(copy)

    rows_scr[TOKENS : TOKENS + RIM, :] = after[...]

    def unconv(d, lanes):
        rows_scr[0:TOKENS, lanes] = d
        v = taps[RIM : RIM + 1, lanes] * d
        for k in range(RIM):
            v += taps[k : k + 1, lanes] * rows_scr[RIM - k : RIM - k + TOKENS, lanes]
        return v

    for n in range(PARTS):
        lanes = part(n)
        gx[:, lanes] = unconv(dpre[:, lanes], lanes)
        send(gx.at[:, lanes], gx_out.at[:, lanes])
    gb[...] = unconv(dpre_bc[:, :STATE], B_LANES)
    send(gb, gb_out)
    gc[...] = unconv(dpre_bc[:, STATE:], C_LANES)
    send(gc, gc_out)
    wait(out)


VMEM = pl.BlockSpec(memory_space=pltpu.VMEM)
HBM = pl.BlockSpec(memory_space=pltpu.HBM)


def call(kernel, ins, outs, scratch=(), sems=(), flops=0, mib=20):
    shapes = [jax.ShapeDtypeStruct(s, d) for s, d, _ in outs]
    moved = sum(a.size * a.dtype.itemsize for a, _ in ins) + sum(s.size * s.dtype.itemsize for s in shapes)
    return pl.pallas_call(
        kernel,
        out_shape=shapes,
        in_specs=[w for _, w in ins],
        out_specs=[w for _, _, w in outs],
        scratch_shapes=[pltpu.VMEM(s, d) for s, d in scratch] + [pltpu.SemaphoreType.DMA((n,)) for n in sems],
        compiler_params=pltpu.CompilerParams(vmem_limit_bytes=mib * 1024 * 1024),
        cost_estimate=pl.CostEstimate(flops=flops, bytes_accessed=moved, transcendentals=0),
    )(*[a for a, _ in ins])


def along_row(block, shift):
    return lax.ppermute(
        block, "context", [(SIDE * y + x, SIDE * y + (x + shift) % SIDE) for y in range(SIDE) for x in range(SIDE)]
    )


def along_column(block, shift):
    return lax.ppermute(
        block, "context", [(SIDE * y + x, SIDE * ((y + shift) % SIDE) + x) for y in range(SIDE) for x in range(SIDE)]
    )


def on_device(
    x_raw, b_raw, c_raw, dt_raw, dt_bias, a_log, skip_gain, conv_x, conv_b, conv_c, grad_y
):
    wide, slim, bc, narrow = (TOKENS, WIDTH), (HEADS, TOKENS), (TOKENS, 2 * STATE), (TOKENS, STATE)
    rim16, row = (16, WIDTH), (1, HEADS)
    dt_bias, a_log, skip_gain = (v.reshape(row) for v in (dt_bias, a_log, skip_gain))

    def near(*arrays):
        return [(a, VMEM) for a in arrays]

    (edge,) = call(
        edge_kernel, [(a, HBM) for a in (x_raw, b_raw, c_raw)], [((RIM, ALL), bf16, VMEM)], [((16, ALL), bf16)], [3],
        mib=60, flops=2_000_000_000,
    )
    before = lax.ppermute(edge, "context", [(i, i + 1) for i in range(RANKS - 1)])
    sg, pre16, end16, ge16, taps, total, cum, step, columns = call(
        first_kernel,
        near(x_raw, grad_y, b_raw, c_raw, dt_raw, dt_bias, a_log, conv_x, conv_b, conv_c),
        [((2, STATE, WIDTH), f32, VMEM), ((16, ALL), f32, VMEM), (rim16, f32, VMEM), (rim16, f32, VMEM),
         ((4, ALL), f32, VMEM), ((HEADS, 8, 128), f32, VMEM), (slim, f32, VMEM), (slim, f32, VMEM),
         ((TOKENS, 128), bf16, VMEM)],
        [((TOKENS + 8, ALL), f32)],
        flops=2_000_000_000,
    )
    message = ((QUARTER, CHUNK, 128), bf16, VMEM)
    pays = call(
        send_kernel, near(before, sg, pre16, end16, ge16, taps, total), [message] * SIDE, [(rim16, f32), (rim16, f32)]
    )

    def block(group, after_this, shared):
        first_pair, count = sum(GROUP_PAIRS[:group]), GROUP_PAIRS[group]
        own = (TOKENS, count * 128)
        outs = [(own, f32, VMEM)] * 3 + [((2,) + own, bf16, VMEM)] * 2
        square = (TOKENS, 128)
        carried = [((3, SUB, SUB), f32, VMEM), (square, f32, VMEM), (square, f32, VMEM)]
        if group == 0:
            outs += [
                (bc, f32, VMEM), (bc, f32, VMEM), ((4, SUB, SUB), f32, VMEM), ((2, SUB, 2 * SUB), bf16, VMEM),
                ((TOKENS, 256), f32, VMEM), ((256, 1152), bf16, VMEM), ((2 * HEADS, 8, TOKENS), f32, VMEM),
                (square, f32, VMEM),
            ]
        if group == len(GROUP_PAIRS) - 1:
            outs += [(bc, f32, VMEM), ((2,) + slim, f32, VMEM)]
        return call(
            functools.partial(block_kernel, first_pair, count),
            near(x_raw, grad_y, b_raw, c_raw, before, taps, cum, step, skip_gain, after_this, *shared),
            outs + carried,
            [((TOKENS + 8, ALL), f32)],
            flops=4_000_000_000,
        )

    got = [pays[0]] + [along_row(pays[shift], shift) for shift in (1, 2, 3)]
    done = block(0, pays[0], ())
    group0, shared = done[:5], done[5:]
    *sends, s_all, g_all, d_all = call(
        row_kernel,
        near(*got, shared[-1]),
        [((QUARTER, ROWMSG, 128), bf16, VMEM)] * (SIDE - 1)
        + [((SIDE, QUARTER, HEAD_DIM, 128), f32, VMEM)] * 2 + [((SIDE, QUARTER, 8, 128), f32, VMEM)],
    )
    rows = [along_column(sends[shift - 1], shift) for shift in (1, 2, 3)]
    done = block(1, d_all, shared)
    group1, sums_so_far = done[:5], done[5:]
    answers = call(
        column_kernel,
        near(*rows, s_all, g_all, d_all, sums_so_far[-1]),
        [message] * SIDE,
        [((SIDE, QUARTER, HEAD_DIM, 128), f32), ((SIDE, QUARTER, 8, 128), f32), ((SIDE, QUARTER, CHUNK, 128), bf16)],
    )
    backs = [answers[0]] + [along_row(answers[shift], shift) for shift in (1, 2, 3)]
    done = block(2, answers[0], [*shared[:8], *sums_so_far])
    group2, (dbc, sums) = done[:5], done[5:7]
    bcs, slope_bc = shared[:2]
    groups = (group0, group1, group2)
    cat = ((2 * STATE, WIDTH), bf16)
    e_cat, f_cat, rim = call(
        rim_kernel,
        near(*backs, bcs, slope_bc, dbc, end16, *[g[n] for n in (1, 2, 3, 4) for g in groups]),
        [(*cat, VMEM), (*cat, VMEM), ((RIM, ALL), f32, VMEM)],
    )
    after = lax.ppermute(rim, "context", [(i, i - 1) for i in range(1, RANKS)])
    y_out, dpre, dpre_bc, grad_dt = call(
        main_kernel,
        near(e_cat, f_cat, columns, bcs, dbc, slope_bc, sums, cum, step, dt_raw, dt_bias, a_log, *[a for g in groups for a in g]),
        [(wide, f32, HBM), (wide, f32, VMEM), (bc, f32, VMEM), (slim, f32, HBM)],
        [(wide, f32), (slim, f32)],
        [PARTS + 1],
        flops=2_000_000_000,
    )
    grad_x, grad_b, grad_c = call(
        settle_kernel,
        near(dpre, dpre_bc, after, taps),
        [(wide, f32, HBM), (narrow, f32, HBM), (narrow, f32, HBM)],
        [((TOKENS + 8, ALL), f32), (wide, f32), (narrow, f32), (narrow, f32)],
        [PARTS + 2],
    )
    return (y_out, grad_x, grad_b, grad_c, grad_dt)


def solution(mesh):
    tokens = P(("dp", "context"), "tensor")
    heads = P("tensor", ("dp", "context"))
    one, taps = P("tensor"), P(None, "tensor")
    return jax.shard_map(
        on_device,
        mesh=mesh,
        in_specs=(tokens, tokens, tokens, heads, one, one, one, taps, taps, taps, tokens),
        out_specs=(tokens, tokens, tokens, tokens, heads),
        check_vma=False,
    )
```

```python
import functools

import jax
import jax.numpy as jnp
from jax import lax
from jax.experimental import pallas as pl
from jax.experimental.pallas import tpu as pltpu
from jax.sharding import PartitionSpec as P

f32 = jnp.float32
bf16 = jnp.bfloat16

TOKENS = 256
SUB = 128
HEADS = 16
HEAD_DIM = 64
STATE = 128
WIDTH = HEADS * HEAD_DIM
PAIRS = HEADS // 2
RIM = 3
RANKS = 16
SIDE = 4
QUARTER = HEADS // SIDE
ROWMSG = 80
CHUNK = 144
ALL = WIDTH + 2 * STATE
PART = 256
PARTS = WIDTH // PART
NEG = -1e30
CODE_SPAN = 248.0

NN = ((1,), (0,))
NT = ((1,), (1,))
TN = ((0,), (0,))


def dot(a, b, dims=NN):
    return lax.dot_general(a, b, (dims, ((), ())), preferred_element_type=f32)


def split2(v):
    hi = v.astype(bf16)
    return hi, (v - hi.astype(f32)).astype(bf16)


def split3(v):
    hi = v.astype(bf16)
    rest = v - hi.astype(f32)
    mid = rest.astype(bf16)
    return hi, mid, (rest - mid.astype(f32)).astype(bf16)


def dot3(a, b, dims=NN):
    return dot(a[0], b[0], dims) + dot(a[1], b[0], dims) + dot(a[0], b[1], dims)


def iota(shape, axis):
    return lax.broadcasted_iota(jnp.int32, shape, axis)


def onehot(mask):
    return jnp.where(mask, 1.0, 0.0).astype(bf16)


def to_column(row):
    n = row.shape[1]
    eye = iota((n, n), 0) == iota((n, n), 1)
    return jnp.sum(jnp.where(eye, row, 0.0), axis=1, keepdims=True)


def low_half(shape):
    return iota(shape, 1) < HEAD_DIM


def swap_halves(v):
    return pltpu.roll(v, HEAD_DIM, 1)


def encode(v):
    top = jnp.max(jnp.abs(v), axis=0, keepdims=True)
    scale = (jnp.maximum(top, 1e-30) * 1.01).astype(bf16).astype(f32)
    unit = jnp.abs(v) * (CODE_SPAN / scale)
    size = jnp.exp2(unit - CODE_SPAN / 2)
    return jnp.where(v < 0, -size, size).astype(bf16), scale


def decode(code, scale):
    v = code.astype(f32)
    unit = jnp.log2(jnp.abs(v)) + CODE_SPAN / 2
    size = unit * (scale * (1.0 / CODE_SPAN))
    return jnp.where(v < 0, -size, size)


def split_heads(pair):
    top, bottom = pair[:HEAD_DIM], pair[HEAD_DIM:]
    low = low_half(top.shape)
    return (
        jnp.where(low, top, swap_halves(bottom)),
        jnp.where(low, swap_halves(top), bottom),
    )


def join_heads(first, second):
    low = low_half(first.shape)
    return (
        jnp.where(low, first, swap_halves(second)),
        jnp.where(low, swap_halves(first), second),
    )


def stack_columns(arrays):
    stacked = jnp.concatenate(list(arrays), axis=0)
    parts = [p.astype(f32) for p in split3(stacked)]
    rows = 3 * stacked.shape[0]
    full = 128 if rows <= 128 else 256
    parts.append(jnp.zeros((full - rows, TOKENS), f32))
    return jnp.concatenate(parts, axis=0).T.astype(bf16)


def spread_matrix(count, full, which, first_head, lanes_per_head, lanes):
    r, l = iota((full, lanes), 0), iota((full, lanes), 1)
    rows = r - (r // (count * HEADS)) * (count * HEADS)
    return onehot((r < 3 * count * HEADS) & (rows - l // lanes_per_head == which * HEADS + first_head))


def sum_matrix(rows, offset):
    r, l = iota((rows, 128), 0), iota((rows, 128), 1)
    return onehot(r // HEAD_DIM + offset == l)


def decay_terms(cum, step):
    first = iota(cum.shape, 1) < SUB
    end0 = cum[:, SUB - 1 : SUB]
    end1 = cum[:, TOKENS - 1 : TOKENS]
    inner = jnp.exp(cum)
    outer = jnp.exp(jnp.where(first, end0, end1) - cum) * step
    from_start = jnp.where(first, inner, inner * jnp.exp(end0))
    to_end = jnp.where(first, outer * jnp.exp(end1), outer)
    return inner, outer, from_start, to_end, end0 + end1


def begin(moves, sems):
    copies = [pltpu.make_async_copy(a, b, sems.at[n]) for n, (a, b) in enumerate(moves)]
    for copy in copies:
        copy.start()
    return copies


def wait(copies):
    for copy in copies:
        copy.wait()


def part(n):
    return pl.ds(n * PART, PART)


def silu_of(v):
    return v / (1.0 + jnp.exp(-v))


def slope_of(v):
    gate = 1.0 / (1.0 + jnp.exp(-v))
    return v * gate, gate * (1.0 + v * (1.0 - gate))


def conv_rows(rows_scr, taps, lanes):
    v = taps[0:1] * rows_scr[8 - RIM : 8 - RIM + TOKENS, lanes]
    for k in range(1, RIM + 1):
        v += taps[k : k + 1] * rows_scr[8 - RIM + k : 8 - RIM + k + TOKENS, lanes]
    return v


B_LANES = pl.ds(WIDTH, STATE)
C_LANES = pl.ds(WIDTH + STATE, STATE)


def edge_kernel(x_raw, b_raw, c_raw, dt_bias, a_log, skip, edge, params, scr, rows_scr, sems):
    rows = pl.ds(TOKENS - 16, 16)
    wait(
        begin(
            [
                (x_raw.at[rows, :], scr.at[:, pl.ds(0, WIDTH)]),
                (b_raw.at[rows, :], scr.at[:, B_LANES]),
                (c_raw.at[rows, :], scr.at[:, C_LANES]),
                (dt_bias, rows_scr.at[0]),
                (a_log, rows_scr.at[1]),
                (skip, rows_scr.at[2]),
            ],
            sems,
        )
    )
    edge[...] = scr[...].astype(f32)[16 - RIM :].astype(bf16)
    for n in range(3):
        params[n] = jnp.broadcast_to(rows_scr[n], (8, HEADS))


def first_kernel(
    xs, gs, bs, cs, dts, params, taps_x, taps_b, taps_c,
    sg, pre16, end16, ge16, taps_out, total_out, cum_out, step_out, columns_out,
    rows_scr,
):
    pre = dts[...].astype(f32) + to_column(params[0][0:1])
    step = jnp.maximum(pre, 0.0) + jnp.log1p(jnp.exp(-jnp.abs(pre)))
    log_decay = -jnp.exp(to_column(params[1][0:1])) * step
    r, c = iota((TOKENS, TOKENS), 0), iota((TOKENS, TOKENS), 1)
    upto = onehot((r <= c) & (r // SUB == c // SUB))
    parts = split3(log_decay)
    cum = dot(parts[2], upto) + dot(parts[1], upto) + dot(parts[0], upto)
    _, _, from_start, to_end, total = decay_terms(cum, step)
    columns = stack_columns([from_start, to_end])
    taps_out[:, 0:WIDTH] = taps_x[...]
    taps_out[:, WIDTH : WIDTH + STATE] = taps_b[...]
    taps_out[:, WIDTH + STATE :] = taps_c[...]
    rows_scr[0:8, :] = jnp.zeros((8, ALL), f32)
    known = iota((TOKENS, 128), 0) >= 16
    turned = []
    for raw, taps, lanes in ((bs, taps_b, B_LANES), (cs, taps_c, C_LANES)):
        rows_scr[8:, lanes] = raw[...].astype(f32)
        v = conv_rows(rows_scr, taps[...], lanes)
        pre16[:, lanes] = v[:16]
        turned.append(split2(jnp.where(known, silu_of(v), 0.0).T))
    bt, ct = turned
    for n in range(PARTS):
        lanes = part(n)
        heads = n * PART // HEAD_DIM
        start_x = dot(columns, spread_matrix(2, 128, 0, heads, HEAD_DIM, PART))
        end_x = dot(columns, spread_matrix(2, 128, 1, heads, HEAD_DIM, PART))
        rows_scr[8:, lanes] = xs[:, lanes].astype(f32)
        v = conv_rows(rows_scr, taps_x[:, lanes], lanes)
        pre16[:, lanes] = v[:16]
        end16[:, lanes] = end_x[:16]
        xw = silu_of(v) * end_x
        ge = gs[:, lanes].astype(f32) * start_x
        ge16[:, lanes] = ge[:16]
        sg[0, :, lanes] = dot3(bt, split2(xw))
        sg[1, :, lanes] = dot3(ct, split2(ge))
    cum_out[...] = cum
    step_out[...] = step
    columns_out[...] = columns
    for head in range(HEADS):
        total_out[head] = jnp.broadcast_to(total[head : head + 1], (8, 128))


def quarter(q):
    return pl.ds(pl.multiple_of(q * PART, PART), PART)


def place():
    here = lax.axis_index("context")
    return lax.rem(here, SIDE), lax.div(here, SIDE)


def write_aux(scales, total):
    at = iota((16, 128), 0)
    aux = jnp.where(at == 0, scales[0], scales[-1])
    for m, piece in enumerate(split3(total)):
        aux = jnp.where(at == 2 + m, piece.astype(f32), aux)
    return aux.astype(bf16)


def send_kernel(before, sg, pre16, end16, ge16, taps, total, *refs):
    pays, (xw_scr, ge_scr) = refs[:SIDE], refs[SIDE:]
    halo = before[...].astype(f32)
    v = pre16[...]
    at = iota((16, ALL), 0)
    for row in range(RIM):
        more = taps[0:1] * halo[row : row + 1]
        for k in range(1, RIM - row):
            more += taps[k : k + 1] * halo[row + k : row + k + 1]
        v += jnp.where(at == row, more, 0.0)
    act = silu_of(v)
    xw_scr[...] = act[:, :WIDTH] * end16[...]
    ge_scr[...] = ge16[...]
    b = split2(act[:, WIDTH : WIDTH + STATE])
    c = split2(act[:, WIDTH + STATE :])
    x, _ = place()
    for shift, pay in enumerate(pays):
        q = lax.rem(x + shift, SIDE)
        lanes = quarter(q)
        s = sg[0, :, lanes] + dot3(b, split2(xw_scr[:, lanes]), TN)
        g = sg[1, :, lanes] + dot3(c, split2(ge_scr[:, lanes]), TN)
        for half in range(PART // 128):
            s_heads = split_heads(s[:, half * 128 : half * 128 + 128])
            g_heads = split_heads(g[:, half * 128 : half * 128 + 128])
            for k in range(2):
                slot = 2 * half + k
                s_code, s_scale = encode(s_heads[k])
                g_code, g_scale = encode(g_heads[k])
                pay[slot, 0:64, :] = s_code
                pay[slot, 64:128, :] = g_code
                pay[slot, 128:144, :] = write_aux((s_scale, g_scale), total[q * QUARTER + slot][0:1])


def row_kernel(*refs):
    pays, tick, refs = refs[:SIDE], refs[SIDE], refs[SIDE + 1 :]
    (*sends, s_out, g_out, d_out) = refs
    x, y = place()
    for shift, pay in enumerate(pays):
        source = lax.rem(x - shift + SIDE, SIDE)
        for k in range(QUARTER):
            aux = pay[k, 128:144, :].astype(f32)
            s_out[source, k] = decode(pay[k, 0:64, :], aux[0:1])
            g_out[source, k] = decode(pay[k, 64:128, :], aux[1:2])
            d_out[source, k] = jnp.broadcast_to(aux[2:3] + aux[3:4] + aux[4:5], (8, 128))
    for k in range(QUARTER):
        s_run, g_run = s_out[0, k], g_out[SIDE - 1, k]
        for n in range(1, SIDE):
            s_run = jnp.exp(d_out[n, k][0:1]) * s_run + s_out[n, k]
            m = SIDE - 1 - n
            g_run = jnp.exp(d_out[m, k][0:1]) * g_run + g_out[m, k]
        total = sum(d_out[n, k][0:1] for n in range(SIDE))
        for shift, message in enumerate(sends, 1):
            code, scale = encode(jnp.where(y + shift < SIDE, s_run, g_run))
            message[k, 0:64, :] = code
            message[k, 64:80, :] = write_aux((scale,), total)


def column_kernel(*refs):
    rows, (s_in, g_in, d_in, tick), refs = refs[: SIDE - 1], refs[SIDE - 1 : SIDE + 3], refs[SIDE + 3 :]
    backs, (row_scr, decay_scr, code_scr) = refs[:SIDE], refs[SIDE:]
    x, y = place()
    row_scr[...] = jnp.zeros_like(row_scr)
    decay_scr[...] = jnp.zeros_like(decay_scr)
    for shift, row in enumerate(rows, 1):
        source = lax.rem(y - shift + SIDE, SIDE)
        for k in range(QUARTER):
            aux = row[k, 64:80, :].astype(f32)
            row_scr[source, k] = decode(row[k, 0:64, :], aux[0:1])
            decay_scr[source, k] = jnp.broadcast_to(jnp.exp(aux[2:3] + aux[3:4] + aux[4:5]), (8, 128))
    for k in range(QUARTER):
        e_run = jnp.zeros((HEAD_DIM, 128), f32)
        f_run = jnp.zeros((HEAD_DIM, 128), f32)
        for n in range(SIDE):
            e_run = jnp.where(n < y, decay_scr[n, k][0:1] * e_run + row_scr[n, k], e_run)
            m = SIDE - 1 - n
            f_run = jnp.where(m > y, decay_scr[m, k][0:1] * f_run + row_scr[m, k], f_run)
        scales = [[None, None] for _ in range(SIDE)]
        for n in range(SIDE):
            m = SIDE - 1 - n
            code_scr[n, k, 0:64, :], scales[n][0] = encode(e_run)
            code_scr[m, k, 64:128, :], scales[m][1] = encode(f_run)
            e_run = jnp.exp(d_in[n, k][0:1]) * e_run + s_in[n, k]
            f_run = jnp.exp(d_in[m, k][0:1]) * f_run + g_in[m, k]
        at = iota((16, 128), 0)
        for n in range(SIDE):
            code_scr[n, k, 128:144, :] = jnp.where(at == 0, scales[n][0], scales[n][1]).astype(bf16)
    for shift, back in enumerate(backs):
        back[...] = code_scr[lax.rem(x + shift, SIDE)]


def block_setup(bs, cs, taps, cums, steps, rows_scr, shared):
    bcs, slopes_bc, sc_scr, off_scr, cols_scr, pick_scr, row_scr, diag_scr, ds, acc, dg = shared

    def rows(parts, s):
        return tuple(p[s * SUB : s * SUB + SUB] for p in parts)

    cum, step = cums[...], steps[...]
    shifted = cum - jnp.log(step)
    for head in range(HEADS):
        row_scr[head] = jnp.broadcast_to(cum[head : head + 1], (8, TOKENS))
        row_scr[HEADS + head] = jnp.broadcast_to(shifted[head : head + 1], (8, TOKENS))
    inner, outer, from_start, to_end, _ = decay_terms(cum, step)
    stacked = []
    for n, v in enumerate((cum, shifted, inner, outer, step, from_start, to_end)):
        stacked += [p.astype(f32) for p in split3(v)[: 3 if n < 2 else 2]]
    cols_scr[...] = jnp.concatenate(stacked, axis=0).T
    r, l = iota((256, 256), 0), iota((256, 256), 1)
    same = r % 2 == l // 128
    pick_scr[:, 0:256] = onehot((r < 48) & same)
    pick_scr[:, 256:512] = onehot((r >= 48) & (r < 96) & same)
    r, l = iota((256, 128), 0), iota((256, 128), 1)
    same = r % 2 == l // HEAD_DIM
    for n in range(5):
        pick_scr[:, 512 + 128 * n : 640 + 128 * n] = onehot(((r - 96) // 32 == n) & (r >= 96) & same)
    for n, (raw, lanes) in enumerate(((bs, B_LANES), (cs, C_LANES))):
        rows_scr[8:, lanes] = raw[...].astype(f32)
        act, slope = slope_of(conv_rows(rows_scr, taps[:, lanes], lanes))
        bcs[:, n * STATE : n * STATE + STATE] = act
        slopes_bc[:, n * STATE : n * STATE + STATE] = slope
    b, c = bcs[:, :STATE], bcs[:, STATE:]
    r, l = iota((SUB, SUB), 0), iota((SUB, SUB), 1)
    b2, c2 = split2(b), split2(c)

    for s in range(2):
        sc_scr[s] = jnp.where(r > l, dot3(rows(c2, s), rows(b2, s), NT), 0.0)
        sc_scr[2 + s] = jnp.where(l > r, dot3(rows(b2, s), rows(c2, s), NT), 0.0)
    off_scr[0] = jnp.concatenate(split2(dot3(rows(c2, 1), rows(b2, 0), NT)), axis=1)
    off_scr[1] = jnp.concatenate(split2(dot3(rows(b2, 0), rows(c2, 1), NT)), axis=1)
    ds[...] = jnp.zeros_like(ds)
    acc[...] = jnp.zeros_like(acc)
    diag = jnp.broadcast_to(jnp.sum(b * c, axis=1, keepdims=True), (TOKENS, 128))
    diag_scr[...] = diag
    dg[...] = jnp.zeros_like(dg)


def block_pairs(first_pair, count, xs, gs, taps, skip, outs, rows_scr, shared):
    ys, dxs, slopes, xws, ges = outs
    _, _, sc_scr, off_scr, cols_scr, pick_scr, row_scr, diag_scr, ds, acc, dg = shared
    r, l = iota((SUB, SUB), 0), iota((SUB, SUB), 1)
    low = low_half((SUB, 128))
    zero = jnp.zeros((SUB, 128), bf16)
    pair_of = (iota((TOKENS, 256), 1) % HEADS) // 2
    column = iota((256, 128), 1) - (iota((256, 128), 0) // HEAD_DIM) % 2

    def twice(hi, lo):
        return jnp.concatenate([jnp.concatenate([hi, lo], axis=1), jnp.concatenate([hi, zero], axis=1)], axis=0)

    def fold(v):
        return v[:, :128] + v[:, 128:]

    def pair_step(pair):
        lanes = pl.ds(pair * 128, 128)
        local = pl.ds((pair - first_pair) * 128, 128)
        head = 2 * pair
        rows_scr[8:, lanes] = xs[:, lanes].astype(f32)
        x, slope = slope_of(conv_rows(rows_scr, taps[:, lanes], lanes))
        slopes[:, local] = slope
        g = gs[:, lanes]
        gf = g.astype(f32)
        xh, xl = split2(x)
        cols = jnp.where(pair_of == pair, cols_scr[...], 0.0).astype(bf16)
        cum_cols = dot(cols, pick_scr[:, 0:256])
        shifted_cols = dot(cols, pick_scr[:, 256:512])
        inner_x, outer_x = (dot(cols, pick_scr[:, a : a + 128]) for a in (512, 640))
        step_x, start_x, end_x = (dot(cols, pick_scr[:, a : a + 128]) for a in (768, 896, 1024))
        for n, piece in enumerate(split2(x * end_x)):
            xws[n, :, local] = piece
        for n, piece in enumerate(split2(gf * start_x)):
            ges[n, :, local] = piece
        y_parts, dx_parts = [], []
        for s in range(2):
            at = slice(s * SUB, s * SUB + SUB)
            xh_s, xl_s, g_s = xh[at], xl[at], g[at]
            ms, ts, decays = [], [], []
            for k in range(2):
                row_cum = row_scr[head + k][0:1, at]
                row_shift = row_scr[HEADS + head + k][0:1, at]
                col_cum = cum_cols[at, k * 128 : k * 128 + 128]
                col_shift = shifted_cols[at, k * 128 : k * 128 + 128]
                decay = jnp.exp(jnp.where(r > l, col_cum - row_shift, NEG))
                decay_t = jnp.exp(jnp.where(l > r, row_cum - col_shift, NEG))
                decays.append(decay)
                ms.append(jnp.concatenate(split2(sc_scr[s] * decay), axis=1))
                ts.append(jnp.concatenate(split2(sc_scr[2 + s] * decay_t), axis=1))
            y2 = fold(dot(jnp.concatenate(ms, axis=0), twice(xh_s, xl_s)))
            dx2 = dot(jnp.concatenate(ts, axis=0), jnp.concatenate([g_s, g_s], axis=0))
            gf_s = g_s.astype(f32)
            g0 = jnp.where(low, gf_s, 0.0).astype(bf16)
            g1 = jnp.where(low, 0.0, gf_s).astype(bf16)
            g01 = jnp.concatenate([g0, g1], axis=0)
            dm = dot(jnp.concatenate([g01, g01], axis=1), jnp.concatenate([xh_s, xl_s], axis=1), NT)
            ds[s] += dm[:SUB] * decays[0] + dm[SUB:] * decays[1]
            y_parts.append(jnp.where(low, y2[:SUB], y2[SUB:]))
            dx_parts.append(jnp.where(low, dx2[:SUB], dx2[SUB:]))
        xwh, xwl = split2(x[:SUB] * outer_x[:SUB])
        geh, gel = split2(gf[SUB:] * inner_x[SUB:])
        y_parts[1] += inner_x[SUB:] * fold(dot(off_scr[0], twice(xwh, xwl)))
        dx_parts[0] += outer_x[:SUB] * fold(dot(off_scr[1], twice(geh, gel)))
        ds[2] += dot(jnp.concatenate([geh, gel], axis=1), jnp.concatenate([xwh, xwh], axis=1), NT) + dot(geh, xwl, NT)
        y = jnp.concatenate(y_parts, axis=0)
        dx = jnp.concatenate(dx_parts, axis=0)
        xg = x * gf
        xdx = x * dx
        total = acc[...]
        for n, v in enumerate((gf * y - xdx, xdx, xg)):
            hot = onehot(column == n * HEADS + head)
            total += dot(jnp.concatenate(split2(v), axis=1), hot)
        acc[...] = total
        dg[...] += step_x * xg
        direct = jnp.where(low_half((TOKENS, 128)), skip[2][0:1, head : head + 1], skip[2][0:1, head + 1 : head + 2]) + diag_scr[...] * step_x
        ys[:, local] = y + direct * x
        dxs[:, local] = dx + direct * gf

    for pair in range(first_pair, first_pair + count):
        pair_step(pair)


def block_finish(steps, dbcs, sums, shared):
    bcs, _, _, _, _, _, _, diag_scr, ds, acc, dg = shared
    step = steps[...]
    b, c = bcs[:, :STATE], bcs[:, STATE:]
    b2, c2 = split2(b), split2(c)
    r, l = iota((SUB, SUB), 0), iota((SUB, SUB), 1)

    def rows(parts, s):
        return tuple(p[s * SUB : s * SUB + SUB] for p in parts)

    d_diag = jnp.sum(dg[...], axis=1, keepdims=True)
    db = d_diag * c
    dc = d_diag * b
    for s in range(2):
        d = jnp.where(r > l, ds[s], 0.0)
        d2 = split2(d)
        t2 = split2(d.T)
        at = slice(s * SUB, s * SUB + SUB)
        dc_s = dc[at] + dot3(d2, rows(b2, s))
        db_s = db[at] + dot3(t2, rows(c2, s))
        if s == 0:
            db_s += dot3(split2(ds[2].T), rows(c2, 1))
        else:
            dc_s += dot3(split2(ds[2]), rows(b2, 0))
        dbcs[at, :STATE] = db_s
        dbcs[at, STATE:] = dc_s
    turned = acc[...].T
    sums[0] = turned[0:HEADS]
    sums[1] = turned[HEADS : 2 * HEADS] / step + diag_scr[...].T[0:1] * turned[2 * HEADS : 3 * HEADS]


def block_kernel(first_pair, count, *refs):
    (xs, gs, bs, cs, before, taps, cums, steps, skip, _), refs = refs[:10], refs[10:]
    rows_scr, refs = refs[-1], refs[:-1]
    rows_scr[8 - RIM : 8, :] = before[...].astype(f32)
    if first_pair == 0:
        outs, shared = refs[:5], refs[5:]
        block_setup(bs, cs, taps, cums, steps, rows_scr, shared)
    else:
        (*kept, ds_in, acc_in, dg_in), refs = refs[:11], refs[11:]
        outs, (ds, acc, dg) = refs[:5], refs[-3:]
        ds[...] = ds_in[...]
        acc[...] = acc_in[...]
        dg[...] = dg_in[...]
        shared = (*kept, ds, acc, dg)
    block_pairs(first_pair, count, xs, gs, taps, skip, outs, rows_scr, shared)
    if first_pair + count == PAIRS:
        block_finish(steps, refs[5], refs[6], shared)


def wide_product(a2, cat, lanes):
    return dot(jnp.concatenate([a2[0], a2[0]], axis=1), cat[:, lanes]) + dot(a2[1], cat[:STATE, lanes])


GROUP_PAIRS = (4, 2, 2)


def columns_of(refs, n, *lead):
    pieces = []
    for pair in range(2 * n, 2 * n + 2):
        group = 0
        while pair >= GROUP_PAIRS[group]:
            pair -= GROUP_PAIRS[group]
            group += 1
        pieces.append(refs[group][(*lead, slice(pair * 128, pair * 128 + 128))])
    return jnp.concatenate(pieces, axis=1)


def rim_kernel(*refs):
    backs, refs = refs[:SIDE], refs[SIDE:]
    (bc, slope_bc, dbc, end16), refs = refs[:4], refs[4:]
    dxs, slopes, xws, ges, (e_cat, f_cat, rim) = refs[:3], refs[3:6], refs[6:9], refs[9:12], refs[12:]
    x, _ = place()
    for shift, back in enumerate(backs):
        q = lax.rem(x - shift + SIDE, SIDE)
        blocks = [[], []]
        for half in range(PART // 128):
            codes = []
            for k in range(2):
                slot = 2 * half + k
                aux = back[slot, 128:144, :].astype(f32)
                codes.append((decode(back[slot, 0:64, :], aux[0:1]), decode(back[slot, 64:128, :], aux[1:2])))
            for n in range(2):
                blocks[n].append(jnp.concatenate(join_heads(codes[0][n], codes[1][n]), axis=0))
        for n, cat in enumerate((e_cat, f_cat)):
            hi, lo = split2(jnp.concatenate(blocks[n], axis=1))
            cat[:STATE, quarter(q)] = hi
            cat[STATE:, quarter(q)] = lo
    b2 = split2(bc[0:16, :STATE])
    for n in range(PARTS):
        top = slice(0, 16)
        d = columns_of(dxs, n, top) + end16[:, part(n)] * wide_product(b2, f_cat, part(n))
        d = d * columns_of(slopes, n, top)
        rim[:, n * PART : n * PART + PART] = d[:RIM]
    for n, (v, cat) in enumerate(((xws, f_cat), (ges, e_cat))):
        hi, lo = (jnp.concatenate([w[m, 0:16, :] for w in v], axis=1) for m in range(2))
        both = dot(hi, cat[...], NT)
        d = both[:, :STATE] + both[:, STATE:] + dot(lo, cat[:STATE], NT)
        cut = slice(n * STATE, n * STATE + STATE)
        d = (dbc[0:16, cut] + d) * slope_bc[0:16, cut]
        rim[:, WIDTH + n * STATE : WIDTH + n * STATE + STATE] = d[:RIM]


def main_kernel(*refs):
    (e_cat, f_cat, columns, bc, dbc, slope_bc, sums, cums, steps, dts, params), refs = refs[:11], refs[11:]
    groups, (y_out, dpre, dpre_bc, dt_out, ys, gdt, out_sems) = refs[:15], refs[15:]
    b2, c2 = split2(bc[:, :STATE]), split2(bc[:, STATE:])
    grads = [[jnp.zeros((TOKENS, PART), f32), jnp.zeros((TOKENS, STATE), f32)] for _ in range(2)]
    total = jnp.zeros((TOKENS, 128), f32)
    both = jnp.zeros((8, 128), f32)
    whole = slice(None)
    out = []
    for n in range(PARTS):
        lanes = part(n)
        heads = n * PART // HEAD_DIM
        y_in, dx, slope = (columns_of(groups[k::5], n, whole) for k in range(3))
        xw, ge = ([columns_of(groups[k::5], n, m, whole) for m in range(2)] for k in (3, 4))
        start_x = dot(columns[...], spread_matrix(2, 128, 0, heads, HEAD_DIM, PART))
        end_x = dot(columns[...], spread_matrix(2, 128, 1, heads, HEAD_DIM, PART))
        ce = wide_product(c2, e_cat, lanes)
        bf = wide_product(b2, f_cat, lanes)
        ys[:, lanes] = y_in + start_x * ce
        copy = pltpu.make_async_copy(ys.at[:, lanes], y_out.at[:, lanes], out_sems.at[n])
        copy.start()
        out.append(copy)
        dpre[:, lanes] = (dx + end_x * bf) * slope
        for grad, v, cat in zip(grads, (xw, ge), (f_cat, e_cat)):
            grad[0] += dot(v[0], cat[:, lanes], NT)
            grad[1] += dot(v[1], cat[:STATE, lanes], NT)
        for v, product, offset in ((xw, bf, 0), (ge, ce, HEADS)):
            hi, lo = split2((v[0].astype(f32) + v[1].astype(f32)) * product)
            hot = sum_matrix(PART, offset + heads)
            total += dot(hi, hot) + dot(lo, hot)
        e = e_cat[:STATE, lanes].astype(f32) + e_cat[STATE:, lanes].astype(f32)
        f = f_cat[:STATE, lanes].astype(f32) + f_cat[STATE:, lanes].astype(f32)
        hi, lo = split2(jnp.broadcast_to(jnp.sum(e * f, axis=0, keepdims=True), (8, PART)))
        hot = sum_matrix(PART, heads)
        both += dot(hi, hot) + dot(lo, hot)
    for n, grad in enumerate(grads):
        cut = slice(n * STATE, n * STATE + STATE)
        d = dbc[:, cut] + grad[0][:, :STATE] + grad[0][:, STATE:] + grad[1]
        dpre_bc[:, cut] = d * slope_bc[:, cut]
    turned = total.T
    later, kept = turned[0:HEADS], turned[HEADS : 2 * HEADS]
    r, c = iota((TOKENS, TOKENS), 0), iota((TOKENS, TOKENS), 1)
    suffix = onehot(r >= c)
    prefix = onehot(r < c)

    def summed(v, tri):
        hi, mid, lo = split3(v)
        return dot(lo, tri) + dot(mid, tri) + dot(hi, tri)

    cum, step = cums[...], steps[...]
    ends = jnp.exp(cum[:, SUB - 1 : SUB] + cum[:, TOKENS - 1 : TOKENS])
    d_decay = summed(sums[0] + kept, suffix) + summed(later, prefix) + ends * to_column(both[0:1, 0:HEADS])
    d_step = sums[1] + later / step - jnp.exp(to_column(params[1][0:1])) * d_decay
    pre = dts[...].astype(f32) + to_column(params[0][0:1])
    gdt[...] = d_step / (1.0 + jnp.exp(-pre))
    out.append(pltpu.make_async_copy(gdt, dt_out, out_sems.at[PARTS]))
    out[-1].start()
    wait(out)


def settle_kernel(dpre, dpre_bc, after, taps, gx_out, gb_out, gc_out, rows_scr, gx, gb, gc, out_sems):
    out = []

    def send(src, dst):
        copy = pltpu.make_async_copy(src, dst, out_sems.at[len(out)])
        copy.start()
        out.append(copy)

    rows_scr[TOKENS : TOKENS + RIM, :] = after[...]

    def unconv(d, lanes):
        rows_scr[0:TOKENS, lanes] = d
        v = taps[RIM : RIM + 1, lanes] * d
        for k in range(RIM):
            v += taps[k : k + 1, lanes] * rows_scr[RIM - k : RIM - k + TOKENS, lanes]
        return v

    for n in range(PARTS):
        lanes = part(n)
        gx[:, lanes] = unconv(dpre[:, lanes], lanes)
        send(gx.at[:, lanes], gx_out.at[:, lanes])
    gb[...] = unconv(dpre_bc[:, :STATE], B_LANES)
    send(gb, gb_out)
    gc[...] = unconv(dpre_bc[:, STATE:], C_LANES)
    send(gc, gc_out)
    wait(out)


VMEM = pl.BlockSpec(memory_space=pltpu.VMEM)
HBM = pl.BlockSpec(memory_space=pltpu.HBM)


def call(kernel, ins, outs, scratch=(), sems=(), flops=0, mib=20):
    shapes = [jax.ShapeDtypeStruct(s, d) for s, d, _ in outs]
    moved = sum(a.size * a.dtype.itemsize for a, _ in ins) + sum(s.size * s.dtype.itemsize for s in shapes)
    return pl.pallas_call(
        kernel,
        out_shape=shapes,
        in_specs=[w for _, w in ins],
        out_specs=[w for _, _, w in outs],
        scratch_shapes=[pltpu.VMEM(s, d) for s, d in scratch] + [pltpu.SemaphoreType.DMA((n,)) for n in sems],
        compiler_params=pltpu.CompilerParams(vmem_limit_bytes=mib * 1024 * 1024),
        cost_estimate=pl.CostEstimate(flops=flops, bytes_accessed=moved, transcendentals=0),
    )(*[a for a, _ in ins])


def along_row(block, shift):
    return lax.ppermute(
        block, "context", [(SIDE * y + x, SIDE * y + (x + shift) % SIDE) for y in range(SIDE) for x in range(SIDE)]
    )


def along_column(block, shift):
    return lax.ppermute(
        block, "context", [(SIDE * y + x, SIDE * ((y + shift) % SIDE) + x) for y in range(SIDE) for x in range(SIDE)]
    )


def on_device(
    x_raw, b_raw, c_raw, dt_raw, dt_bias, a_log, skip_gain, conv_x, conv_b, conv_c, grad_y
):
    wide, slim, bc, narrow = (TOKENS, WIDTH), (HEADS, TOKENS), (TOKENS, 2 * STATE), (TOKENS, STATE)
    rim16, row = (16, WIDTH), (1, HEADS)
    dt_bias, a_log, skip_gain = (v.reshape(row) for v in (dt_bias, a_log, skip_gain))

    def near(*arrays):
        return [(a, VMEM) for a in arrays]

    edge, params = call(
        edge_kernel,
        [(a, HBM) for a in (x_raw, b_raw, c_raw, dt_bias, a_log, skip_gain)],
        [((RIM, ALL), bf16, VMEM), ((3, 8, HEADS), f32, VMEM)],
        [((16, ALL), bf16), ((3, 1, HEADS), f32)],
        [6],
        flops=2_000_000_000,
        mib=60,
    )
    before = lax.ppermute(edge, "context", [(i, i + 1) for i in range(RANKS - 1)])
    sg, pre16, end16, ge16, taps, total, cum, step, columns = call(
        first_kernel,
        near(x_raw, grad_y, b_raw, c_raw, dt_raw, params, conv_x, conv_b, conv_c),
        [((2, STATE, WIDTH), f32, VMEM), ((16, ALL), f32, VMEM), (rim16, f32, VMEM), (rim16, f32, VMEM),
         ((4, ALL), f32, VMEM), ((HEADS, 8, 128), f32, VMEM), (slim, f32, VMEM), (slim, f32, VMEM),
         ((TOKENS, 128), bf16, VMEM)],
        [((TOKENS + 8, ALL), f32)],
        flops=2_000_000_000,
    )
    message = ((QUARTER, CHUNK, 128), bf16, VMEM)
    pays = call(
        send_kernel, near(before, sg, pre16, end16, ge16, taps, total), [message] * SIDE, [(rim16, f32), (rim16, f32)]
    )

    def block(group, after_this, shared):
        first_pair, count = sum(GROUP_PAIRS[:group]), GROUP_PAIRS[group]
        own = (TOKENS, count * 128)
        outs = [(own, f32, VMEM)] * 3 + [((2,) + own, bf16, VMEM)] * 2
        square = (TOKENS, 128)
        carried = [((3, SUB, SUB), f32, VMEM), (square, f32, VMEM), (square, f32, VMEM)]
        if group == 0:
            outs += [
                (bc, f32, VMEM), (bc, f32, VMEM), ((4, SUB, SUB), f32, VMEM), ((2, SUB, 2 * SUB), bf16, VMEM),
                ((TOKENS, 256), f32, VMEM), ((256, 1152), bf16, VMEM), ((2 * HEADS, 8, TOKENS), f32, VMEM),
                (square, f32, VMEM),
            ]
        if group == len(GROUP_PAIRS) - 1:
            outs += [(bc, f32, VMEM), ((2,) + slim, f32, VMEM)]
        return call(
            functools.partial(block_kernel, first_pair, count),
            near(x_raw, grad_y, b_raw, c_raw, before, taps, cum, step, params, after_this, *shared),
            outs + carried,
            [((TOKENS + 8, ALL), f32)],
            flops=4_000_000_000,
        )

    got = [pays[0]] + [along_row(pays[shift], shift) for shift in (1, 2, 3)]
    done = block(0, pays[0], ())
    group0, shared = done[:5], done[5:]
    *sends, s_all, g_all, d_all = call(
        row_kernel,
        near(*got, shared[-1]),
        [((QUARTER, ROWMSG, 128), bf16, VMEM)] * (SIDE - 1)
        + [((SIDE, QUARTER, HEAD_DIM, 128), f32, VMEM)] * 2 + [((SIDE, QUARTER, 8, 128), f32, VMEM)],
    )
    rows = [along_column(sends[shift - 1], shift) for shift in (1, 2, 3)]
    done = block(1, d_all, shared)
    group1, sums_so_far = done[:5], done[5:]
    answers = call(
        column_kernel,
        near(*rows, s_all, g_all, d_all, sums_so_far[-1]),
        [message] * SIDE,
        [((SIDE, QUARTER, HEAD_DIM, 128), f32), ((SIDE, QUARTER, 8, 128), f32), ((SIDE, QUARTER, CHUNK, 128), bf16)],
    )
    backs = [answers[0]] + [along_row(answers[shift], shift) for shift in (1, 2, 3)]
    done = block(2, answers[0], [*shared[:8], *sums_so_far])
    group2, (dbc, sums) = done[:5], done[5:7]
    bcs, slope_bc = shared[:2]
    groups = (group0, group1, group2)
    cat = ((2 * STATE, WIDTH), bf16)
    e_cat, f_cat, rim = call(
        rim_kernel,
        near(*backs, bcs, slope_bc, dbc, end16, *[g[n] for n in (1, 2, 3, 4) for g in groups]),
        [(*cat, VMEM), (*cat, VMEM), ((RIM, ALL), f32, VMEM)],
    )
    after = lax.ppermute(rim, "context", [(i, i - 1) for i in range(1, RANKS)])
    y_out, dpre, dpre_bc, grad_dt = call(
        main_kernel,
        near(e_cat, f_cat, columns, bcs, dbc, slope_bc, sums, cum, step, dt_raw, params, *[a for g in groups for a in g]),
        [(wide, f32, HBM), (wide, f32, VMEM), (bc, f32, VMEM), (slim, f32, HBM)],
        [(wide, f32), (slim, f32)],
        [PARTS + 1],
        flops=2_000_000_000,
    )
    grad_x, grad_b, grad_c = call(
        settle_kernel,
        near(dpre, dpre_bc, after, taps),
        [(wide, f32, HBM), (narrow, f32, HBM), (narrow, f32, HBM)],
        [((TOKENS + 8, ALL), f32), (wide, f32), (narrow, f32), (narrow, f32)],
        [PARTS + 2],
    )
    return (y_out, grad_x, grad_b, grad_c, grad_dt)


def solution(mesh):
    tokens = P(("dp", "context"), "tensor")
    heads = P("tensor", ("dp", "context"))
    one, taps = P("tensor"), P(None, "tensor")
    return jax.shard_map(
        on_device,
        mesh=mesh,
        in_specs=(tokens, tokens, tokens, heads, one, one, one, taps, taps, taps, tokens),
        out_specs=(tokens, tokens, tokens, tokens, heads),
        check_vma=False,
    )
```
